512 devices in a mesh: dp: 8 (over y_hi, core), ep: 64 (over y_lo, x, z).
Axes of the slice: x: 4, y: 8 (y_hi: 4, y_lo: 2; y = y_hi * 2 + y_lo), z: 8, core: 2. Of those that a mesh axis runs over, the one named last changes fastest.
Arguments:
- latent_cache: bfloat16 [64, 16, 512, 576], P('ep', 'dp'), may hold values from -6 to 6
- lengths: int32 [64, 16], P(None, 'dp'), may hold values from 2 to 512
- new_home: int32 [64, 16], P(None, 'dp'), may hold values from 0 to 63, as said below
- queries: bfloat16 [2, 64, 16, 128, 576], P(None, 'ep', 'dp'), may hold values from -32 to 32
- new_latent: bfloat16 [2, 64, 16, 576], P(None, 'ep', 'dp'), may hold values from -6 to 6
- hidden: bfloat16 [2, 64, 16, 3584], P(None, 'ep', 'dp'), may hold values from -6 to 6
- routes: int32 [2, 64, 16, 8], P(None, 'ep', 'dp'), may hold values from 0 to 63, all different within a row; in each aligned block of 16 rows (0 to 15, 16 to 31, ..., all dimensions but the last counted through in order) at most 4 rows name the same one
- route_logits: bfloat16 [2, 64, 16, 8], P(None, 'ep', 'dp'), may hold values from -8 to 8
- w_gate: bfloat16 [64, 3584, 1024], P('ep', None, 'dp'), may hold values from -0.09375 to 0.09375
- w_up: bfloat16 [64, 3584, 1024], P('ep', None, 'dp'), may hold values from -0.09375 to 0.09375
- w_down: bfloat16 [64, 1024, 3584], P('ep', 'dp'), may hold values from -0.1875 to 0.1875
Outputs:
- attended: bfloat16 [2, 64, 16, 128, 512], P(None, 'ep', 'dp')
- moe_out: bfloat16 [2, 64, 16, 3584], P(None, 'ep', 'dp')
The draws below stay inside these ranges and needn't reach their ends.
Inputs may be any that keep to these rules, and one draw needn't show every extreme that they name: `routes`: in each step, the 16 requests of one ep index name any one expert in at most 4 of their choices, and this bound is reached. For each request index c, new_home[., c] exchanges exactly two ep indices and leaves every other one in place, so new_home[new_home[e, c], c] == e; the two indices lie 64 // 2 apart for even c and 1 apart (modulo 64) for odd c.
All inputs are finite; a program needn't handle non-finite values.
Results may differ from the reference program's by a relative error of at most 0.0057.
Values may be sent and summed in bfloat16 or wider, within the bound.
No kernel may reach another device: no remote copies, remote signals or barrier semaphores. Data moves between devices by JAX's collectives and lax.ppermute only.
A program may use at most 128 MiB of HBM per device.

```python
import math
import jax
import jax.numpy as jnp
import numpy as np
from jax import lax

D = 3584
FF = 1024
HEADS = 128
KV_RANK = 512
ROPE = 64
HEAD_QK = 192
TOP = 8
STEPS = 2
CACHE = 512
EXPERTS = 64
COLROWS = 16
CAP = 4
N_DP = 8


def integer_parts(key):
    subkeys = jax.random.split(jax.random.fold_in(key, 5), 5)
    heavy_rank = jax.random.randint(subkeys[0], (EXPERTS, 1), 0, 6) == 0
    long_rows = jax.random.randint(subkeys[1], (EXPERTS, COLROWS), CACHE // 2, CACHE + 1)
    short_rows = jax.random.randint(subkeys[2], (EXPERTS, COLROWS), 2, CACHE // 4 + 2)
    flat_lengths = jnp.where(heavy_rank, long_rows, short_rows).reshape(-1)
    total_rows = EXPERTS * COLROWS
    first_spot = jax.random.randint(subkeys[3], (), 0, total_rows)
    second_spot = (first_spot + 1 + jax.random.randint(subkeys[4], (), 0, total_rows - 1)) % total_rows
    spots = jnp.arange(total_rows)
    flat_lengths = jnp.where(spots == first_spot, CACHE, flat_lengths)
    flat_lengths = jnp.where(spots == second_spot, 2, flat_lengths)
    lengths = flat_lengths.reshape(EXPERTS, COLROWS).astype(jnp.int32)
    rank_ids = jnp.arange(EXPERTS, dtype=jnp.int32)[:, None]
    long_score = lengths * EXPERTS + (EXPERTS - 1 - rank_ids)
    heavy_pick = jnp.argmax(long_score, 0).astype(jnp.int32)
    request_ids = jnp.arange(COLROWS, dtype=jnp.int32)
    offset = jnp.where(request_ids % 2 == 0, EXPERTS // 2, 1).astype(jnp.int32)
    light_pick = ((heavy_pick + offset) % EXPERTS).astype(jnp.int32)
    homes = jnp.where(rank_ids == heavy_pick[None, :], light_pick[None, :], jnp.where(rank_ids == light_pick[None, :], heavy_pick[None, :], rank_ids))
    return (lengths, homes.astype(jnp.int32))


def draw_lengths(key, part):
    return integer_parts(key)[0]


def draw_new_home(key, part):
    return integer_parts(key)[1]


def float_parts(key):
    subkeys = jax.random.split(jax.random.fold_in(key, 9), 3)
    lat_width = KV_RANK + ROPE
    cache_shape = (EXPERTS, COLROWS, CACHE, lat_width)
    fresh_shape = (STEPS, EXPERTS, COLROWS, lat_width)
    query_shape = (STEPS, EXPERTS, COLROWS, HEADS, lat_width)
    cache_rows = jax.random.truncated_normal(subkeys[0], -6.0, 6.0, cache_shape, jnp.float32)
    fresh_rows = jax.random.truncated_normal(subkeys[1], -6.0, 6.0, fresh_shape, jnp.float32)
    query_rows = 0.9 * jax.random.truncated_normal(subkeys[2], -6.0, 6.0, query_shape, jnp.float32) + 0.1 * fresh_rows[:, :, :, None, :]
    return (cache_rows.astype(jnp.bfloat16), fresh_rows.astype(jnp.bfloat16), query_rows.astype(jnp.bfloat16))


def draw_latent_cache(key, part):
    return float_parts(key)[0]


def draw_new_latent(key, part):
    return float_parts(key)[1]


def draw_queries(key, part):
    return float_parts(key)[2]


def block_levels(rng, extent, cuts, least, largest):
    gain = 1.0
    for position, parts in cuts:
        heights = jax.random.uniform(jax.random.fold_in(jax.random.fold_in(rng, 6), position), (parts,), jnp.float32, least / len(cuts), largest / len(cuts))
        gain = gain * jnp.repeat(jnp.exp(heights), extent[position] // parts).reshape((-1,) + (1,) * (len(extent) - 1 - position))
    return gain


def assign_block(key, own, number, rows, count, top, most, lean):
    ranking = jax.random.permutation(key, count)
    crowded, ordinary = load_shares(count, rows * top, most, lean, True), load_shares(count, rows * top, most, lean, False)
    places = jnp.arange(count)

    def named(sizes, rotation):
        used = int((sizes > 0).sum())
        fixed = max(1, used // 4)
        shifted = fixed + (places - fixed + rotation * (used - fixed)) % max(1, count - fixed)
        return jnp.zeros((count,), jnp.int32).at[ranking[jnp.where(places < fixed, places, shifted)]].set(jnp.asarray(sizes, jnp.int32))

    sizes = jnp.where(number % 4 == 0, named(crowded, number // 4), named(ordinary, number - number // 4 - 1))
    mixed = jax.random.permutation(jax.random.fold_in(own, 3), count)
    giver, receiver = mixed[0:count // 2 * 2:2], mixed[1:count // 2 * 2:2]
    margin = jnp.minimum(sizes[giver] - 1, most - sizes[receiver]) // 2
    margin = jnp.where((giver == ranking[0]) | (receiver == ranking[0]) | (sizes[receiver] == 0), 0, jnp.maximum(margin, 0))
    shifted = jax.random.randint(jax.random.fold_in(own, 4), (count // 2,), 0, 1 << 20) % (margin + 1)
    sizes = sizes.at[giver].add(-shifted).at[receiver].add(shifted)
    members = jnp.searchsorted(jnp.cumsum(sizes), jnp.arange(rows * top), side="right").astype(jnp.int32)
    listing = members.reshape(top, rows).T
    listing = listing[jax.random.permutation(jax.random.fold_in(own, 1), rows)]
    rotation = jax.random.randint(jax.random.fold_in(own, 2), (rows, 1), 0, top)
    return jnp.take_along_axis(listing, (jnp.arange(top)[None, :] + rotation) % top, axis=1)


def load_shares(amount, total, limit, skew, full):
    portions = [(1 << 20) // math.isqrt(rank ** skew) + 1 for rank in range(1, amount + 1)]
    largest = limit if full else min(limit, max(-(-total // amount), total * portions[0] // sum(portions)))
    least = 1 if total - largest >= amount - 1 else 0
    holding, rest = [largest] + [least] * (amount - 1), total - largest - least * (amount - 1)
    while rest > 0:
        candidates = [i for i in range(1, amount) if holding[i] < largest] or [i for i in range(1, amount) if holding[i] < limit]
        whole, remaining = sum([portions[i] for i in candidates]), rest
        for i in candidates:
            extra = min(limit - holding[i], max(1, remaining * portions[i] // whole), rest)
            holding[i] = holding[i] + extra
            rest = rest - extra
    return np.array(holding)


def gaussian(rng, shape, scale, most, cuts=(), kind=jnp.bfloat16):
    result = scale * jax.random.normal(rng, shape, jnp.float32)
    if cuts:
        result = result * block_levels(rng, shape, cuts, -0.22, 0.18)
    return jnp.clip(result, -most, most).astype(kind)


def setup_inputs(seed: int = 0) -> dict:
    key_of = jax.random.split(jax.random.key(seed), 12)
    latent_cache = draw_latent_cache(jax.random.fold_in(key_of[11], 71), 0)
    lengths = draw_lengths(jax.random.fold_in(key_of[11], 71), 0)
    new_home = draw_new_home(jax.random.fold_in(key_of[11], 71), 0)
    queries = draw_queries(jax.random.fold_in(key_of[11], 71), 0)
    new_latent = draw_new_latent(jax.random.fold_in(key_of[11], 71), 0)
    hidden = gaussian(key_of[5], (STEPS, EXPERTS, COLROWS, D), 1.0, 6.0, ((1, 64), (2, 8)))
    routes_keys = jax.random.split(jax.random.fold_in(key_of[6], 1), STEPS * EXPERTS * COLROWS // COLROWS)
    routes_turns = jax.random.permutation(jax.random.fold_in(key_of[6], 3), STEPS * EXPERTS * COLROWS // COLROWS)
    routes = jax.vmap(lambda own, number: assign_block(jax.random.fold_in(key_of[6], 2), own, number, COLROWS, EXPERTS, TOP, CAP, 2))(routes_keys, routes_turns).reshape((STEPS, EXPERTS, COLROWS, TOP))
    route_logits = gaussian(key_of[7], (STEPS, EXPERTS, COLROWS, TOP), 2.0, 8.0, ((1, 64), (2, 8)))
    w_gate = gaussian(key_of[8], (EXPERTS, D, FF), D ** -0.5, 0.09375, ((0, 64), (2, 8)))
    w_up = gaussian(key_of[9], (EXPERTS, D, FF), D ** -0.5, 0.09375, ((0, 64), (2, 8)))
    w_down = gaussian(key_of[10], (EXPERTS, FF, D), FF ** -0.5, 0.1875, ((0, 64), (1, 8)))
    return dict(latent_cache=latent_cache, lengths=lengths, new_home=new_home, queries=queries, new_latent=new_latent, hidden=hidden, routes=routes, route_logits=route_logits, w_gate=w_gate, w_up=w_up, w_down=w_down)


def attend_one(query_rows, cache_rows, fresh_rows, length):
    step_count, head_count, lat_width = query_rows.shape
    softmax_scale = HEAD_QK ** -0.5
    flat_query = query_rows.reshape(step_count * head_count, lat_width)
    cache_scores = jnp.dot(flat_query, cache_rows.T, preferred_element_type=jnp.float32) * softmax_scale
    key_place = jnp.arange(cache_rows.shape[0], dtype=jnp.int32)
    cache_scores = jnp.where(key_place[None, :] < length, cache_scores, -jnp.inf)
    fresh_scores = jnp.dot(flat_query, fresh_rows.T, preferred_element_type=jnp.float32) * softmax_scale
    row_step = jnp.arange(step_count * head_count, dtype=jnp.int32) // head_count
    fresh_step = jnp.arange(step_count, dtype=jnp.int32)
    fresh_scores = jnp.where(fresh_step[None, :] <= row_step[:, None], fresh_scores, -jnp.inf)
    all_scores = jnp.concatenate([cache_scores, fresh_scores], 1)
    row_max = jnp.max(all_scores, 1, keepdims=True)
    weights = jnp.exp(all_scores - row_max)
    probs_all = (weights / jnp.sum(weights, 1, keepdims=True)).astype(jnp.bfloat16)
    key_values = jnp.concatenate([cache_rows, fresh_rows], 0)[:, :KV_RANK]
    served = jnp.dot(probs_all, key_values, preferred_element_type=jnp.float32).astype(jnp.bfloat16)
    return served.reshape(step_count, head_count, KV_RANK)


def expert(items):
    expert_rows, gate_w, up_w, down_w = items
    gate_part = jnp.dot(expert_rows, gate_w, preferred_element_type=jnp.float32)
    up_part = jnp.dot(expert_rows, up_w, preferred_element_type=jnp.float32)
    hidden_units = lax.optimization_barrier((jax.nn.silu(gate_part) * up_part).astype(jnp.bfloat16))
    slices = hidden_units.astype(jnp.float32).reshape(-1, N_DP, FF // N_DP).transpose(1, 0, 2)
    down_slices = down_w.astype(jnp.float32).reshape(N_DP, FF // N_DP, D)
    slice_out = jnp.einsum("jrf,jfd->jrd", slices, down_slices, precision=lax.Precision.HIGHEST)
    rounded = lax.optimization_barrier(slice_out.astype(jnp.bfloat16))
    return jnp.sum(rounded.astype(jnp.float32), 0)


def reference(latent_cache, lengths, new_home, queries, new_latent, hidden, routes, route_logits, w_gate, w_up, w_down):
    query_cols = jnp.transpose(queries, (1, 2, 0, 3, 4))
    fresh_cols = jnp.transpose(new_latent, (1, 2, 0, 3))

    def per_rank(items):
        cache_rank, length_rank, query_rank, fresh_rank = items
        return jax.vmap(attend_one)(query_rank, cache_rank, fresh_rank, length_rank)

    results = lax.map(per_rank, (latent_cache, lengths, query_cols, fresh_cols))
    relocated = results[new_home, jnp.arange(COLROWS, dtype=jnp.int32)[None, :]]
    attended = jnp.transpose(relocated, (2, 0, 1, 3, 4))

    sigmoid_part = jax.nn.sigmoid(route_logits.astype(jnp.float32))
    gate_weights = 2.5 * sigmoid_part / jnp.sum(sigmoid_part, -1, keepdims=True)
    rank_ids = jnp.arange(EXPERTS, dtype=jnp.int32)
    outputs = []
    for number in range(STEPS):
        flat_routes = routes[number].reshape(EXPERTS, COLROWS * TOP)
        onehot = (flat_routes[:, :, None] == rank_ids[None, None, :]).astype(jnp.int32)
        slot_rank = jnp.sum(jnp.cumsum(onehot, 1) * onehot, 2) - 1
        slot_index = flat_routes * CAP + slot_rank
        tokens = jnp.repeat(hidden[number], TOP, axis=1)
        buffer = jnp.zeros((EXPERTS, EXPERTS * CAP, D), jnp.bfloat16)
        buffer = buffer.at[rank_ids[:, None], slot_index].set(tokens)
        by_expert = buffer.reshape(EXPERTS, EXPERTS, CAP, D).transpose(1, 0, 2, 3).reshape(EXPERTS, EXPERTS * CAP, D)
        expert_out = lax.map(expert, (by_expert, w_gate, w_up, w_down)).reshape(EXPERTS, EXPERTS, CAP, D)
        picked = expert_out[flat_routes, rank_ids[:, None], slot_rank]
        weighted = picked.reshape(EXPERTS, COLROWS, TOP, D) * gate_weights[number][..., None]
        outputs.append(jnp.sum(weighted, 2).astype(jnp.bfloat16))
    moe_out = jnp.stack(outputs, 0)
    return attended, moe_out
```

```python
import functools

import jax
import jax.numpy as jnp
from jax import lax
from jax.experimental import pallas as pl
from jax.experimental.pallas import tpu as pltpu
from jax.sharding import Mesh
from jax.sharding import PartitionSpec as P

KV_RANK = 512
HEAD_QK = 192
CAP = 4
EP = ("yl", "x", "z")
DP = ("yh", "c")
BF = jnp.bfloat16
F32 = jnp.float32
PARAMS = pltpu.CompilerParams(vmem_limit_bytes=48 * 1024 * 1024)


def dot(a, b, dims=((1,), (0,))):
    return lax.dot_general(a, b, (dims, ((), ())), preferred_element_type=F32)


def iota(shape, dim):
    return lax.broadcasted_iota(jnp.int32, shape, dim)


def vmem(n):
    return [pl.BlockSpec(memory_space=pltpu.VMEM)] * n


def attend_kernel(len_ref, query_ref, cache_ref, fresh_ref, out0_ref, out1_ref, keys_ref):
    steps, _, requests, heads, width = query_ref.shape
    cached = cache_ref.shape[2]
    total = keys_ref.shape[0]
    rows = steps * heads
    column = iota((rows, total), 1)
    row_step = iota((rows, total), 0) // heads
    for request, out_ref in zip(range(requests), (out0_ref, out1_ref)):
        keys_ref[:cached] = cache_ref[0, request]
        place = iota((total - cached, width), 0)
        tail = jnp.zeros((total - cached, width), F32)
        for step in range(steps):
            row = fresh_ref[step, 0, request : request + 1, :].astype(F32)
            tail = jnp.where(place == step, row, tail)
        keys_ref[cached:] = tail.astype(BF)
        query = query_ref[:, 0, request].reshape(rows, width)
        keys = keys_ref[...]
        scores = dot(query, keys, ((1,), (1,))) * (HEAD_QK**-0.5)
        old = column < len_ref[request]
        new = (column >= cached) & (column - cached <= row_step)
        scores = jnp.where(old | new, scores, -jnp.inf)
        weights = jnp.exp(scores - jnp.max(scores, 1, keepdims=True))
        probs = (weights / jnp.sum(weights, 1, keepdims=True)).astype(BF)
        served = dot(probs, keys[:, :KV_RANK]).astype(BF)
        out_ref[...] = served.reshape(steps, heads, KV_RANK)


def attend(length, queries, cache, fresh):
    steps, _, _, heads, width = queries.shape
    out = jax.ShapeDtypeStruct((steps, heads, KV_RANK), BF)
    return pl.pallas_call(
        attend_kernel,
        out_shape=(out, out),
        in_specs=[pl.BlockSpec(memory_space=pltpu.SMEM), *vmem(3)],
        out_specs=tuple(vmem(2)),
        scratch_shapes=[pltpu.VMEM((cache.shape[2] + 128, width), BF)],
        compiler_params=PARAMS,
        name="attend",
    )(length, queries, cache, fresh)


def dispatch_kernel(tokens_ref, send_ref, mix_ref):
    rows = tokens_ref.shape[0]
    slots, half = send_ref.shape
    width = 2 * half
    tail = tokens_ref[:, width:].astype(F32)
    top = tail.shape[1] // 2
    sigmoid = jax.nn.sigmoid(tail[:, top:])
    gates = 2.5 * sigmoid / jnp.sum(sigmoid, 1, keepdims=True)
    slot = iota((rows, slots), 1)
    expert = (slot // 8).astype(F32)
    named = jnp.zeros((rows, slots), F32)
    gate = jnp.zeros((rows, slots), F32)
    for k in range(top):
        hit = tail[:, k : k + 1] == expert
        named = jnp.where(hit, 1.0, named)
        gate = jnp.where(hit, gates[:, k : k + 1], gate)
    before = (iota((rows, rows), 1) < iota((rows, rows), 0)).astype(F32)
    earlier = dot(before.astype(BF), named.astype(BF))
    chosen = (named > 0) & (earlier == (slot % 4).astype(F32))
    left = chosen & (slot % 8 < 4)
    right = chosen & (slot % 8 >= 4)
    picks = (left.astype(F32).astype(BF), right.astype(F32).astype(BF))
    over_rows = ((0,), (0,))
    send = dot(picks[0], tokens_ref[:, :half], over_rows)
    send = send + dot(picks[1], tokens_ref[:, half:width], over_rows)
    send_ref[...] = send.astype(BF)
    high = gate.astype(BF).astype(F32)
    low = gate - high
    mix = [jnp.where(side, part, 0.0) for part in (high, low) for side in (left, right)]
    mix_ref[...] = jnp.concatenate(mix, 0).astype(BF)


def dispatch(tokens, slots, half):
    return pl.pallas_call(
        dispatch_kernel,
        out_shape=(
            jax.ShapeDtypeStruct((slots, half), BF),
            jax.ShapeDtypeStruct((4 * tokens.shape[0], slots), BF),
        ),
        in_specs=vmem(1),
        out_specs=tuple(vmem(2)),
        compiler_params=PARAMS,
        name="dispatch",
    )(tokens)


def hidden_kernel(rows_ref, own_ref, peer_ref, out_ref):
    slots, half = rows_ref.shape
    units = own_ref.shape[1] // 2
    rows = rows_ref[...]
    parts = []
    for ref in (own_ref, peer_ref):
        upper = dot(rows, ref[:half])
        lower = dot(rows, ref[half:])
        both = upper + pltpu.roll(lower, slots - 4, 0)
        gate, up = both[:, :units], both[:, units:]
        parts.append(gate / (1.0 + jnp.exp(-gate)) * up)
    value = jnp.concatenate(parts, 1)
    value = jnp.where(iota(value.shape, 0) % 8 < 4, value, 0.0).astype(BF)
    row, slot = iota((slots // 2, slots), 0), iota((slots // 2, slots), 1)
    pick = (slot == row // 4 * 8 + row % 4).astype(F32).astype(BF)
    out_ref[...] = dot(pick, value).astype(BF)


def hidden_units(rows, own, peer):
    return pl.pallas_call(
        hidden_kernel,
        out_shape=jax.ShapeDtypeStruct((rows.shape[0] // 2, own.shape[1]), BF),
        in_specs=vmem(3),
        out_specs=vmem(1)[0],
        compiler_params=PARAMS,
        name="hidden_units",
    )(rows, own, peer)


def down_kernel(h0, h1, h2, h3, own_ref, peer_ref, out_ref):
    slots, part = out_ref.shape
    total = None
    for number, ref in enumerate((h0, h1, h2, h3)):
        weights = jnp.concatenate([own_ref[number], peer_ref[number]], 0)
        term = dot(ref[...], weights)
        total = term if total is None else total + term
    value = total.astype(BF)
    rest = value.shape[1] - part
    slot, row = iota((slots, slots // 2), 0), iota((slots, slots // 2), 1)
    match = slot // 8 * 4 + slot % 4 == row
    left = (match & (slot % 8 < 4)).astype(F32).astype(BF)
    right = (match & (slot % 8 >= 4)).astype(F32).astype(BF)
    first, second = dot(left, value[:, :part]), dot(right, value[:, part:])
    out_ref[:, :rest] = (first[:, :rest] + second).astype(BF)
    out_ref[:, rest:] = first[:, rest:].astype(BF)


def down(hs, own, peer, part):
    rows = hs[0].shape[0]
    return pl.pallas_call(
        down_kernel,
        out_shape=jax.ShapeDtypeStruct((2 * rows, part), BF),
        in_specs=vmem(6),
        out_specs=vmem(1)[0],
        compiler_params=PARAMS,
        name="down",
    )(*hs, own, peer)


def combine_kernel(mix_ref, back_ref, out_ref):
    rows = mix_ref.shape[0] // 4
    part = back_ref.shape[1]
    rest = out_ref.shape[1] - part
    value = dot(mix_ref[...], back_ref[...])
    value = value[: 2 * rows] + value[2 * rows :]
    out_ref[:, :part] = value[:rows].astype(BF)
    out_ref[:, part:] = value[rows:, :rest].astype(BF)


def combine(mix, back, width):
    return pl.pallas_call(
        combine_kernel,
        out_shape=jax.ShapeDtypeStruct((mix.shape[0] // 4, width), BF),
        in_specs=vmem(2),
        out_specs=vmem(1)[0],
        compiler_params=PARAMS,
        name="combine",
    )(mix, back)


def exchange(x, axes):
    return lax.all_to_all(x, axes, split_axis=0, concat_axis=0, tiled=True)


def shifted(x, axes, by):
    size = lax.axis_size(axes)
    return lax.ppermute(x, axes, [(i, (i + by) % size) for i in range(size)])


def shards(
    latent_cache,
    lengths,
    new_home,
    queries,
    new_latent,
    hidden,
    routes,
    route_logits,
    w_gate,
    w_up,
    w_down,
):
    experts = lax.axis_size(EP)
    yh_size = lax.axis_size("yh")
    own_rank = lax.axis_index(EP)
    yh = lax.axis_index("yh")
    steps, _, requests, width = hidden.shape
    half = width // 2
    chunk = width // yh_size
    part = (chunk // 2 + 127) // 128 * 128
    slots = experts * 2 * CAP

    packed = jnp.concatenate([hidden, routes.astype(BF), route_logits], -1)[:, 0]
    packed = jnp.broadcast_to(packed[None], (yh_size, *packed.shape))
    tokens = exchange(packed.reshape(-1, *packed.shape[2:]), DP)
    tokens = tokens.reshape(-1, tokens.shape[-1])
    send, mix = dispatch(tokens, slots, half)
    arrived = exchange(send.reshape(experts, 2 * CAP, half), EP).reshape(slots, half)

    own_w = jnp.concatenate([w_gate[0], w_up[0]], 1)
    peer_w = shifted(own_w, "c", 1)
    down_blocks = [
        lax.dynamic_slice_in_dim(w_down[0], (yh + s) % yh_size * chunk, chunk, 1)
        for s in range(yh_size)
    ]
    own_down = jnp.stack([shifted(x, "yh", s) if s else x for s, x in enumerate(down_blocks)])
    peer_down = shifted(own_down, "c", 1)

    served0, served1 = attend(lengths[own_rank], queries, latent_cache, new_latent)
    far = shifted(served0, EP, experts // 2)
    lower = shifted(served1, EP, 1)
    upper = shifted(served1, EP, -1)
    home = new_home[own_rank]
    result0 = jnp.where(home[0] == own_rank, served0, far)
    result1 = jnp.where(
        home[1] == own_rank,
        served1,
        jnp.where(home[1] == (own_rank + 1) % experts, upper, lower),
    )
    attended = jnp.stack([result0, result1], 1)[:, None]

    h = hidden_units(arrived, own_w, peer_w)
    hs = [h, *(shifted(h, "yh", s) for s in range(1, yh_size))]
    out = down(hs, own_down, peer_down, part)
    back = exchange(out.reshape(experts, 2 * CAP, part), EP).reshape(slots, part)
    mixed = combine(mix, back, chunk)
    final = exchange(mixed.reshape(-1, requests, chunk), DP)
    final = final.reshape(yh_size, steps, requests, chunk).transpose(1, 2, 0, 3)
    moe_out = final.reshape(steps, 1, requests, width)
    return attended, moe_out


def solution(mesh):
    torus = Mesh(mesh.devices.reshape(4, 2, 2, 4, 8), ("yh", "c", "yl", "x", "z"))
    placed = (
        P(EP, DP, None, None),
        P(None, DP),
        P(None, DP),
        P(None, EP, DP, None, None),
        P(None, EP, DP, None),
        P(None, EP, DP, None),
        P(None, EP, DP, None),
        P(None, EP, DP, None),
        P(EP, None, DP),
        P(EP, None, DP),
        P(EP, DP, None),
    )
    return jax.shard_map(
        shards,
        mesh=torus,
        in_specs=placed,
        out_specs=(P(None, EP, DP, None, None), P(None, EP, DP, None)),
        check_vma=False,
    )
```

```python
import functools

import jax
import jax.numpy as jnp
from jax import lax
from jax.experimental import pallas as pl
from jax.experimental.pallas import tpu as pltpu
from jax.sharding import Mesh
from jax.sharding import PartitionSpec as P

KV_RANK = 512
HEAD_QK = 192
CAP = 4
EP = ("yl", "x", "z")
DP = ("yh", "c")
BF = jnp.bfloat16
F32 = jnp.float32
PARAMS = pltpu.CompilerParams(vmem_limit_bytes=48 * 1024 * 1024)


def dot(a, b, dims=((1,), (0,))):
    return lax.dot_general(a, b, (dims, ((), ())), preferred_element_type=F32)


def iota(shape, dim):
    return lax.broadcasted_iota(jnp.int32, shape, dim)


def vmem(n):
    return [pl.BlockSpec(memory_space=pltpu.VMEM)] * n


def attend_kernel(len_ref, query_ref, cache_ref, fresh_ref, out0_ref, out1_ref, keys_ref):
    steps, _, requests, heads, width = query_ref.shape
    cached = cache_ref.shape[2]
    total = keys_ref.shape[0]
    rows = steps * heads
    column = iota((rows, total), 1)
    row_step = iota((rows, total), 0) // heads
    for request, out_ref in zip(range(requests), (out0_ref, out1_ref)):
        keys_ref[:cached] = cache_ref[0, request]
        place = iota((total - cached, width), 0)
        tail = jnp.zeros((total - cached, width), F32)
        for step in range(steps):
            row = fresh_ref[step, 0, request : request + 1, :].astype(F32)
            tail = jnp.where(place == step, row, tail)
        keys_ref[cached:] = tail.astype(BF)
        query = query_ref[:, 0, request].reshape(rows, width)
        keys = keys_ref[...]
        scores = dot(query, keys, ((1,), (1,))) * (HEAD_QK**-0.5)
        old = column < len_ref[request]
        new = (column >= cached) & (column - cached <= row_step)
        scores = jnp.where(old | new, scores, -jnp.inf)
        weights = jnp.exp(scores - jnp.max(scores, 1, keepdims=True))
        probs = (weights / jnp.sum(weights, 1, keepdims=True)).astype(BF)
        served = dot(probs, keys[:, :KV_RANK]).astype(BF)
        out_ref[...] = served.reshape(steps, heads, KV_RANK)


def attend(length, queries, cache, fresh):
    steps, _, _, heads, width = queries.shape
    out = jax.ShapeDtypeStruct((steps, heads, KV_RANK), BF)
    return pl.pallas_call(
        attend_kernel,
        out_shape=(out, out),
        in_specs=[pl.BlockSpec(memory_space=pltpu.SMEM), *vmem(3)],
        out_specs=tuple(vmem(2)),
        scratch_shapes=[pltpu.VMEM((cache.shape[2] + 128, width), BF)],
        compiler_params=PARAMS,
        name="attend",
    )(length, queries, cache, fresh)


def dispatch_kernel(tokens_ref, send_ref, mix_ref):
    rows = tokens_ref.shape[0]
    slots, half = send_ref.shape
    width = 2 * half
    tail = tokens_ref[:, width:].astype(F32)
    top = tail.shape[1] // 2
    sigmoid = jax.nn.sigmoid(tail[:, top:])
    gates = 2.5 * sigmoid / jnp.sum(sigmoid, 1, keepdims=True)
    slot = iota((rows, slots), 1)
    expert = (slot // 8).astype(F32)
    named = jnp.zeros((rows, slots), F32)
    gate = jnp.zeros((rows, slots), F32)
    for k in range(top):
        hit = tail[:, k : k + 1] == expert
        named = jnp.where(hit, 1.0, named)
        gate = jnp.where(hit, gates[:, k : k + 1], gate)
    before = (iota((rows, rows), 1) < iota((rows, rows), 0)).astype(F32)
    earlier = dot(before.astype(BF), named.astype(BF))
    chosen = (named > 0) & (earlier == (slot % 4).astype(F32))
    left = chosen & (slot % 8 < 4)
    right = chosen & (slot % 8 >= 4)
    picks = (left.astype(F32).astype(BF), right.astype(F32).astype(BF))
    over_rows = ((0,), (0,))
    send = dot(picks[0], tokens_ref[:, :half], over_rows)
    send = send + dot(picks[1], tokens_ref[:, half:width], over_rows)
    send_ref[...] = send.astype(BF)
    high = gate.astype(BF).astype(F32)
    low = gate - high
    mix = [jnp.where(side, part, 0.0) for part in (high, low) for side in (left, right)]
    mix_ref[...] = jnp.concatenate(mix, 0).astype(BF)


def dispatch(tokens, slots, half):
    return pl.pallas_call(
        dispatch_kernel,
        out_shape=(
            jax.ShapeDtypeStruct((slots, half), BF),
            jax.ShapeDtypeStruct((4 * tokens.shape[0], slots), BF),
        ),
        in_specs=vmem(1),
        out_specs=tuple(vmem(2)),
        compiler_params=PARAMS,
        name="dispatch",
    )(tokens)


def hidden_kernel(rows_ref, own_ref, peer_ref, out_ref):
    slots, half = rows_ref.shape
    units = own_ref.shape[1] // 2
    rows = rows_ref[...]
    parts = []
    for ref in (own_ref, peer_ref):
        upper = dot(rows, ref[:half])
        lower = dot(rows, ref[half:])
        both = upper + pltpu.roll(lower, slots - 4, 0)
        gate, up = both[:, :units], both[:, units:]
        parts.append(gate / (1.0 + jnp.exp(-gate)) * up)
    value = jnp.concatenate(parts, 1)
    value = jnp.where(iota(value.shape, 0) % 8 < 4, value, 0.0).astype(BF)
    row, slot = iota((slots // 2, slots), 0), iota((slots // 2, slots), 1)
    pick = (slot == row // 4 * 8 + row % 4).astype(F32).astype(BF)
    out_ref[...] = dot(pick, value).astype(BF)


def hidden_units(rows, own, peer):
    return pl.pallas_call(
        hidden_kernel,
        out_shape=jax.ShapeDtypeStruct((rows.shape[0] // 2, own.shape[1]), BF),
        in_specs=vmem(3),
        out_specs=vmem(1)[0],
        compiler_params=PARAMS,
        name="hidden_units",
    )(rows, own, peer)


def down_kernel(h0, h1, h2_top, h2_bottom, h3, own_ref, peer_ref, out_ref):
    slots, part = out_ref.shape
    total = None
    hs = (h0[...], h1[...], jnp.concatenate([h2_top[...], h2_bottom[...]], 0), h3[...])
    for number, h in enumerate(hs):
        weights = jnp.concatenate([own_ref[number], peer_ref[number]], 0)
        term = dot(h, weights)
        total = term if total is None else total + term
    value = total.astype(BF)
    rest = value.shape[1] - part
    slot, row = iota((slots, slots // 2), 0), iota((slots, slots // 2), 1)
    match = slot // 8 * 4 + slot % 4 == row
    left = (match & (slot % 8 < 4)).astype(F32).astype(BF)
    right = (match & (slot % 8 >= 4)).astype(F32).astype(BF)
    first, second = dot(left, value[:, :part]), dot(right, value[:, part:])
    out_ref[:, :rest] = (first[:, :rest] + second).astype(BF)
    out_ref[:, rest:] = first[:, rest:].astype(BF)


def down(hs, own, peer, part):
    rows = hs[0].shape[0]
    return pl.pallas_call(
        down_kernel,
        out_shape=jax.ShapeDtypeStruct((2 * rows, part), BF),
        in_specs=vmem(7),
        out_specs=vmem(1)[0],
        compiler_params=PARAMS,
        name="down",
    )(*hs, own, peer)


def combine_kernel(mix_ref, back_ref, out_ref):
    rows = mix_ref.shape[0] // 4
    part = back_ref.shape[1]
    rest = out_ref.shape[1] - part
    value = dot(mix_ref[...], back_ref[...])
    value = value[: 2 * rows] + value[2 * rows :]
    out_ref[:, :part] = value[:rows].astype(BF)
    out_ref[:, part:] = value[rows:, :rest].astype(BF)


def combine(mix, back, width):
    return pl.pallas_call(
        combine_kernel,
        out_shape=jax.ShapeDtypeStruct((mix.shape[0] // 4, width), BF),
        in_specs=vmem(2),
        out_specs=vmem(1)[0],
        compiler_params=PARAMS,
        name="combine",
    )(mix, back)


def exchange(x, axes):
    return lax.all_to_all(x, axes, split_axis=0, concat_axis=0, tiled=True)


def shifted(x, axes, by):
    size = lax.axis_size(axes)
    return lax.ppermute(x, axes, [(i, (i + by) % size) for i in range(size)])


def shards(
    latent_cache,
    lengths,
    new_home,
    queries,
    new_latent,
    hidden,
    routes,
    route_logits,
    w_gate,
    w_up,
    w_down,
):
    experts = lax.axis_size(EP)
    yh_size = lax.axis_size("yh")
    own_rank = lax.axis_index(EP)
    yh = lax.axis_index("yh")
    steps, _, requests, width = hidden.shape
    half = width // 2
    chunk = width // yh_size
    part = (chunk // 2 + 127) // 128 * 128
    slots = experts * 2 * CAP

    packed = jnp.concatenate([hidden, routes.astype(BF), route_logits], -1)[:, 0]
    packed = jnp.broadcast_to(packed[None], (yh_size, *packed.shape))
    tokens = exchange(packed.reshape(-1, *packed.shape[2:]), DP)
    served = attend(lengths[own_rank], queries, latent_cache, new_latent)
    tokens, served0, served1 = lax.optimization_barrier((tokens, *served))
    tokens = tokens.reshape(-1, tokens.shape[-1])
    send, mix = dispatch(tokens, slots, half)
    send, served0, served1 = lax.optimization_barrier((send, served0, served1))
    arrived = exchange(send.reshape(experts, 2 * CAP, half), EP).reshape(slots, half)

    own_w = jnp.concatenate([w_gate[0], w_up[0]], 1)
    peer_w = shifted(own_w, "c", 1)
    down_blocks = [
        lax.dynamic_slice_in_dim(w_down[0], (yh + s) % yh_size * chunk, chunk, 1)
        for s in range(yh_size)
    ]
    own_down = jnp.stack([shifted(x, "yh", s) if s else x for s, x in enumerate(down_blocks)])
    peer_down = shifted(own_down, "c", 1)

    far = shifted(served0, EP, experts // 2)
    lower = shifted(served1, EP, 1)
    upper = shifted(served1, EP, -1)
    home = new_home[own_rank]
    result0 = jnp.where(home[0] == own_rank, served0, far)
    result1 = jnp.where(
        home[1] == own_rank,
        served1,
        jnp.where(home[1] == (own_rank + 1) % experts, upper, lower),
    )
    attended = jnp.stack([result0, result1], 1)[:, None]

    arrived, peer_w, own_down, peer_down, attended = lax.optimization_barrier(
        (arrived, peer_w, own_down, peer_down, attended)
    )
    h = hidden_units(arrived, own_w, peer_w)
    before, after = shifted(h, "yh", 1), shifted(h, "yh", -1)
    middle = h.shape[0] // 2
    across = (shifted(before[:middle], "yh", 1), shifted(after[middle:], "yh", -1))
    out = down((h, before, *across, after), own_down, peer_down, part)
    back = exchange(out.reshape(experts, 2 * CAP, part), EP).reshape(slots, part)
    mixed = combine(mix, back, chunk)
    final = exchange(mixed.reshape(-1, requests, chunk), DP)
    final = final.reshape(yh_size, steps, requests, chunk).transpose(1, 2, 0, 3)
    moe_out = final.reshape(steps, 1, requests, width)
    return attended, moe_out


def solution(mesh):
    torus = Mesh(mesh.devices.reshape(4, 2, 2, 4, 8), ("yh", "c", "yl", "x", "z"))
    placed = (
        P(EP, DP, None, None),
        P(None, DP),
        P(None, DP),
        P(None, EP, DP, None, None),
        P(None, EP, DP, None),
        P(None, EP, DP, None),
        P(None, EP, DP, None),
        P(None, EP, DP, None),
        P(EP, None, DP),
        P(EP, None, DP),
        P(EP, DP, None),
    )
    return jax.shard_map(
        shards,
        mesh=torus,
        in_specs=placed,
        out_specs=(P(None, EP, DP, None, None), P(None, EP, DP, None)),
        check_vma=False,
    )
```

```python
import functools

import jax
import jax.numpy as jnp
from jax import lax
from jax.experimental import pallas as pl
from jax.experimental.pallas import tpu as pltpu
from jax.sharding import Mesh
from jax.sharding import PartitionSpec as P

KV_RANK = 512
HEAD_QK = 192
CAP = 4
EP = ("yl", "x", "z")
DP = ("yh", "c")
COLUMN = ("yh", "c", "yl")
PLANE = ("x", "z")
BF = jnp.bfloat16
F32 = jnp.float32
PARAMS = pltpu.CompilerParams(vmem_limit_bytes=48 * 1024 * 1024)


def dot(a, b, dims=((1,), (0,))):
    return lax.dot_general(a, b, (dims, ((), ())), preferred_element_type=F32)


def iota(shape, dim):
    return lax.broadcasted_iota(jnp.int32, shape, dim)


def vmem(n):
    return [pl.BlockSpec(memory_space=pltpu.VMEM)] * n


def attend_kernel(len_ref, query_ref, cache_ref, fresh_ref, out0_ref, out1_ref, keys_ref):
    steps, _, requests, heads, width = query_ref.shape
    cached = cache_ref.shape[2]
    total = keys_ref.shape[0]
    rows = steps * heads
    column = iota((rows, total), 1)
    row_step = iota((rows, total), 0) // heads
    for request, out_ref in zip(range(requests), (out0_ref, out1_ref)):
        keys_ref[:cached] = cache_ref[0, request]
        place = iota((total - cached, width), 0)
        tail = jnp.zeros((total - cached, width), F32)
        for step in range(steps):
            row = fresh_ref[step, 0, request : request + 1, :].astype(F32)
            tail = jnp.where(place == step, row, tail)
        keys_ref[cached:] = tail.astype(BF)
        query = query_ref[:, 0, request].reshape(rows, width)
        keys = keys_ref[...]
        scores = dot(query, keys, ((1,), (1,))) * (HEAD_QK**-0.5)
        old = column < len_ref[request]
        new = (column >= cached) & (column - cached <= row_step)
        scores = jnp.where(old | new, scores, -jnp.inf)
        weights = jnp.exp(scores - jnp.max(scores, 1, keepdims=True))
        probs = (weights / jnp.sum(weights, 1, keepdims=True)).astype(BF)
        served = dot(probs, keys[:, :KV_RANK]).astype(BF)
        out_ref[...] = served.reshape(steps, heads, KV_RANK)


def attend(length, queries, cache, fresh):
    steps, _, _, heads, width = queries.shape
    out = jax.ShapeDtypeStruct((steps, heads, KV_RANK), BF)
    return pl.pallas_call(
        attend_kernel,
        out_shape=(out, out),
        in_specs=[pl.BlockSpec(memory_space=pltpu.SMEM), *vmem(3)],
        out_specs=tuple(vmem(2)),
        scratch_shapes=[pltpu.VMEM((cache.shape[2] + 128, width), BF)],
        compiler_params=PARAMS,
        name="attend",
    )(length, queries, cache, fresh)


def dispatch_kernel(yl_ref, tokens_ref, send_ref, mix_ref):
    rows = tokens_ref.shape[0]
    slots, width = send_ref.shape
    tail = tokens_ref[:, width:].astype(F32)
    top = tail.shape[1] // 2
    sigmoid = jax.nn.sigmoid(tail[:, top:])
    gates = 2.5 * sigmoid / jnp.sum(sigmoid, 1, keepdims=True)
    slot = iota((rows, slots), 1)
    expert = (slot // (2 * CAP) + yl_ref[0] * (slots // (2 * CAP))).astype(F32)
    named = jnp.zeros((rows, slots), F32)
    gate = jnp.zeros((rows, slots), F32)
    for k in range(top):
        hit = tail[:, k : k + 1] == expert
        named = jnp.where(hit, 1.0, named)
        gate = jnp.where(hit, gates[:, k : k + 1], gate)
    this, other = iota((rows, rows), 0), iota((rows, rows), 1)
    before = ((other < this) & (other // 2 % 2 == this // 2 % 2)).astype(F32)
    earlier = dot(before.astype(BF), named.astype(BF))
    chosen = (named > 0) & (earlier == (slot % CAP).astype(F32))
    chosen = chosen & (slot % (2 * CAP) // CAP == iota((rows, slots), 0) // 2 % 2)
    pick = chosen.astype(F32).astype(BF)
    send_ref[...] = dot(pick, tokens_ref[:, :width], ((0,), (0,))).astype(BF)
    high = gate.astype(BF).astype(F32)
    mix = [jnp.where(chosen, part, 0.0) for part in (high, gate - high)]
    mix_ref[...] = jnp.concatenate(mix, 0).astype(BF)


def dispatch(yl, tokens, slots, width):
    return pl.pallas_call(
        dispatch_kernel,
        out_shape=(
            jax.ShapeDtypeStruct((slots, width), BF),
            jax.ShapeDtypeStruct((2 * tokens.shape[0], slots), BF),
        ),
        in_specs=[pl.BlockSpec(memory_space=pltpu.SMEM), *vmem(1)],
        out_specs=tuple(vmem(2)),
        compiler_params=PARAMS,
        name="dispatch",
    )(yl.reshape(1), tokens)


def hidden_kernel(rows_ref, own_ref, peer_ref, out_ref):
    units = own_ref.shape[1] // 2
    rows = rows_ref[...]
    for place, ref in enumerate((own_ref, peer_ref)):
        both = dot(rows, ref[...])
        gate, up = both[:, :units], both[:, units:]
        value = gate / (1.0 + jnp.exp(-gate)) * up
        out_ref[:, place * units : (place + 1) * units] = value.astype(BF)


def hidden_units(rows, own, peer):
    return pl.pallas_call(
        hidden_kernel,
        out_shape=jax.ShapeDtypeStruct((rows.shape[0], own.shape[1]), BF),
        in_specs=vmem(3),
        out_specs=vmem(1)[0],
        compiler_params=PARAMS,
        name="hidden_units",
    )(rows, own, peer)


def down_kernel(yh_ref, h_ref, own_ref, peer_ref, out_ref):
    total = None
    count = h_ref.shape[0]
    for number in range(count):
        weights = jnp.concatenate([own_ref[number], peer_ref[number]], 0)
        term = dot(h_ref[(yh_ref[0] + count - number) % count], weights)
        total = term if total is None else total + term
    out_ref[...] = total.astype(BF)


def down(yh, h, own, peer):
    return pl.pallas_call(
        down_kernel,
        out_shape=jax.ShapeDtypeStruct((h.shape[1], own.shape[2]), BF),
        in_specs=[pl.BlockSpec(memory_space=pltpu.SMEM), *vmem(3)],
        out_specs=vmem(1)[0],
        compiler_params=PARAMS,
        name="down",
    )(yh.reshape(1), h, own, peer)


def combine_kernel(mix_ref, back_ref, out_ref):
    rows = out_ref.shape[0]
    value = dot(mix_ref[...], back_ref[...])
    out_ref[...] = value[:rows] + value[rows:]


def combine(mix, back):
    return pl.pallas_call(
        combine_kernel,
        out_shape=jax.ShapeDtypeStruct((mix.shape[0] // 2, back.shape[1]), F32),
        in_specs=vmem(2),
        out_specs=vmem(1)[0],
        compiler_params=PARAMS,
        name="combine",
    )(mix, back)


def exchange(x, axes):
    return lax.all_to_all(x, axes, split_axis=0, concat_axis=0, tiled=True)


def shifted(x, axes, by):
    size = lax.axis_size(axes)
    return lax.ppermute(x, axes, [(i, (i + by) % size) for i in range(size)])


def shards(
    latent_cache,
    lengths,
    new_home,
    queries,
    new_latent,
    hidden,
    routes,
    route_logits,
    w_gate,
    w_up,
    w_down,
):
    experts = lax.axis_size(EP)
    yh_size, yl_size = lax.axis_size("yh"), lax.axis_size("yl")
    peers = experts // yl_size
    own_rank = lax.axis_index(EP)
    steps, _, requests, width = hidden.shape
    chunk = width // yh_size
    block = yl_size * CAP
    slots = peers * block

    packed = jnp.concatenate([hidden, routes.astype(BF), route_logits], -1)[:, 0]
    packed = jnp.broadcast_to(packed[None, :, None], (yh_size, steps, yl_size, *packed.shape[1:]))
    tokens = exchange(packed.reshape(-1, *packed.shape[3:]), COLUMN)
    served = attend(lengths[own_rank], queries, latent_cache, new_latent)
    tokens, served0, served1 = lax.optimization_barrier((tokens, *served))
    tokens = tokens.reshape(-1, tokens.shape[-1])
    send, mix = dispatch(lax.axis_index("yl"), tokens, slots, width)
    arrived = exchange(send.reshape(peers, block, width), PLANE).reshape(slots, width)

    own_w = jnp.concatenate([w_gate[0], w_up[0]], 1)
    peer_w = shifted(own_w, "c", 1)
    yh = lax.axis_index("yh")
    sent = [
        lax.dynamic_slice_in_dim(w_down[0], (yh + s) % yh_size * chunk, chunk, 1)
        for s in range(yh_size)
    ]
    own_down = jnp.stack([shifted(x, "yh", s) if s else x for s, x in enumerate(sent)])
    peer_down = shifted(own_down, "c", 1)

    far = shifted(served0, EP, experts // 2)
    lower = shifted(served1, EP, 1)
    upper = shifted(served1, EP, -1)
    home = new_home[own_rank]
    result0 = jnp.where(home[0] == own_rank, served0, far)
    result1 = jnp.where(
        home[1] == own_rank,
        served1,
        jnp.where(home[1] == (own_rank + 1) % experts, upper, lower),
    )
    attended = jnp.stack([result0, result1], 1)[:, None]

    arrived, peer_w, own_down, attended = lax.optimization_barrier(
        (arrived, peer_w, own_down, attended)
    )
    h = hidden_units(arrived, own_w, peer_w)
    h = exchange(jnp.broadcast_to(h[None], (yh_size, *h.shape)), "yh")
    out = down(yh, h, own_down, peer_down)
    back = exchange(out.reshape(peers, block, chunk), PLANE).reshape(slots, chunk)
    mixed = combine(mix, back)
    final = exchange(mixed.reshape(-1, requests, chunk), COLUMN)
    final = final.reshape(yh_size, steps, yl_size, requests, chunk).sum(2).astype(BF)
    moe_out = final.transpose(1, 2, 0, 3).reshape(steps, 1, requests, width)
    return attended, moe_out


def solution(mesh):
    torus = Mesh(mesh.devices.reshape(4, 2, 2, 4, 8), ("yh", "c", "yl", "x", "z"))
    placed = (
        P(EP, DP, None, None),
        P(None, DP),
        P(None, DP),
        P(None, EP, DP, None, None),
        P(None, EP, DP, None),
        P(None, EP, DP, None),
        P(None, EP, DP, None),
        P(None, EP, DP, None),
        P(EP, None, DP),
        P(EP, None, DP),
        P(EP, DP, None),
    )
    return jax.shard_map(
        shards,
        mesh=torus,
        in_specs=placed,
        out_specs=(P(None, EP, DP, None, None), P(None, EP, DP, None)),
        check_vma=False,
    )
```

```python
import functools

import jax
import jax.numpy as jnp
from jax import lax
from jax.experimental import pallas as pl
from jax.experimental.pallas import tpu as pltpu
from jax.sharding import Mesh
from jax.sharding import PartitionSpec as P

KV_RANK = 512
HEAD_QK = 192
CAP = 4
EP = ("yl", "x", "z")
DP = ("yh", "c")
COLUMN = ("yh", "c", "yl")
PLANE = ("x", "z")
BF = jnp.bfloat16
F32 = jnp.float32
PARAMS = pltpu.CompilerParams(vmem_limit_bytes=48 * 1024 * 1024)


def dot(a, b, dims=((1,), (0,))):
    return lax.dot_general(a, b, (dims, ((), ())), preferred_element_type=F32)


def iota(shape, dim):
    return lax.broadcasted_iota(jnp.int32, shape, dim)


def vmem(n):
    return [pl.BlockSpec(memory_space=pltpu.VMEM)] * n


def attend_kernel(len_ref, query_ref, cache_ref, fresh_ref, out0_ref, out1_ref, keys_ref):
    steps, _, requests, heads, width = query_ref.shape
    cached = cache_ref.shape[2]
    total = keys_ref.shape[0]
    rows = steps * heads
    column = iota((rows, total), 1)
    row_step = iota((rows, total), 0) // heads
    for request, out_ref in zip(range(requests), (out0_ref, out1_ref)):
        keys_ref[:cached] = cache_ref[0, request]
        place = iota((total - cached, width), 0)
        tail = jnp.zeros((total - cached, width), F32)
        for step in range(steps):
            row = fresh_ref[step, 0, request : request + 1, :].astype(F32)
            tail = jnp.where(place == step, row, tail)
        keys_ref[cached:] = tail.astype(BF)
        query = query_ref[:, 0, request].reshape(rows, width)
        keys = keys_ref[...]
        scores = dot(query, keys, ((1,), (1,))) * (HEAD_QK**-0.5)
        old = column < len_ref[request]
        new = (column >= cached) & (column - cached <= row_step)
        scores = jnp.where(old | new, scores, -jnp.inf)
        weights = jnp.exp(scores - jnp.max(scores, 1, keepdims=True))
        probs = (weights / jnp.sum(weights, 1, keepdims=True)).astype(BF)
        served = dot(probs, keys[:, :KV_RANK]).astype(BF)
        out_ref[...] = served.reshape(steps, heads, KV_RANK)


def attend(length, queries, cache, fresh):
    steps, _, _, heads, width = queries.shape
    out = jax.ShapeDtypeStruct((steps, heads, KV_RANK), BF)
    return pl.pallas_call(
        attend_kernel,
        out_shape=(out, out),
        in_specs=[pl.BlockSpec(memory_space=pltpu.SMEM), *vmem(3)],
        out_specs=tuple(vmem(2)),
        scratch_shapes=[pltpu.VMEM((cache.shape[2] + 128, width), BF)],
        compiler_params=PARAMS,
        name="attend",
    )(length, queries, cache, fresh)


def hbm():
    return pl.BlockSpec(memory_space=pltpu.HBM)


def pack_kernel(hidden_ref, routes_ref, logits_ref, out_ref, rows_ref, done):
    width = hidden_ref.shape[3]
    steps = hidden_ref.shape[0]
    per_core = rows_ref.shape[0] // 4 // steps
    for step in range(steps):
        parts = (routes_ref[step, 0].astype(F32), logits_ref[step, 0].astype(F32))
        tail = jnp.concatenate(parts, -1).astype(BF)
        for peer in range(rows_ref.shape[0]):
            if peer // per_core % steps == step:
                rows_ref[peer, :, :width] = hidden_ref[step, 0]
                rows_ref[peer, :, width:] = tail
    copy = pltpu.make_async_copy(rows_ref, out_ref, done)
    copy.start()
    copy.wait()


def pack(hidden, routes, logits, peers):
    _, _, requests, width = hidden.shape
    shape = (peers, requests, width + routes.shape[3] + logits.shape[3])
    return pl.pallas_call(
        pack_kernel,
        out_shape=jax.ShapeDtypeStruct(shape, BF),
        in_specs=vmem(3),
        out_specs=hbm(),
        scratch_shapes=[pltpu.VMEM(shape, BF), pltpu.SemaphoreType.DMA],
        compiler_params=PARAMS,
        name="pack",
    )(hidden, routes, logits)


def dispatch_kernel(yl_ref, tokens_ref, send_ref, mix_ref, held_ref, done):
    rows = tokens_ref.shape[0]
    slots, width = send_ref.shape
    tail = tokens_ref[:, width:].astype(F32)
    top = tail.shape[1] // 2
    sigmoid = jax.nn.sigmoid(tail[:, top:])
    gates = 2.5 * sigmoid / jnp.sum(sigmoid, 1, keepdims=True)
    slot = iota((rows, slots), 1)
    expert = (slot // (2 * CAP) + yl_ref[0] * (slots // (2 * CAP))).astype(F32)
    named = jnp.zeros((rows, slots), F32)
    gate = jnp.zeros((rows, slots), F32)
    for k in range(top):
        hit = tail[:, k : k + 1] == expert
        named = jnp.where(hit, 1.0, named)
        gate = jnp.where(hit, gates[:, k : k + 1], gate)
    this, other = iota((rows, rows), 0), iota((rows, rows), 1)
    before = ((other < this) & (other // 2 % 2 == this // 2 % 2)).astype(F32)
    earlier = dot(before.astype(BF), named.astype(BF))
    chosen = (named > 0) & (earlier == (slot % CAP).astype(F32))
    chosen = chosen & (slot % (2 * CAP) // CAP == iota((rows, slots), 0) // 2 % 2)
    pick = chosen.astype(F32).astype(BF)
    copies = []
    for part in range(0, slots, 128):
        span = slice(part, part + 128)
        sent = dot(pick[:, span], tokens_ref[:, :width], ((0,), (0,)))
        held_ref[span] = sent.astype(BF)
        copy = pltpu.make_async_copy(held_ref.at[span], send_ref.at[span], done.at[part // 128])
        copy.start()
        copies.append(copy)
    high = gate.astype(BF).astype(F32)
    mix = [jnp.where(chosen, part, 0.0) for part in (high, gate - high)]
    mix_ref[...] = jnp.concatenate(mix, 0).astype(BF)
    for copy in copies:
        copy.wait()


def dispatch(yl, tokens, slots, width):
    return pl.pallas_call(
        dispatch_kernel,
        out_shape=(
            jax.ShapeDtypeStruct((slots, width), BF),
            jax.ShapeDtypeStruct((2 * tokens.shape[0], slots), BF),
        ),
        in_specs=[pl.BlockSpec(memory_space=pltpu.SMEM), *vmem(1)],
        out_specs=(hbm(), *vmem(1)),
        scratch_shapes=[
            pltpu.VMEM((slots, width), BF),
            pltpu.SemaphoreType.DMA((slots // 128,)),
        ],
        compiler_params=PARAMS,
        name="dispatch",
    )(yl.reshape(1), tokens)


def hidden_kernel(rows_ref, own_ref, peer_ref, out_ref, held_ref, done):
    units = own_ref.shape[1] // 2
    rows = rows_ref[...]
    for place, ref in enumerate((own_ref, peer_ref)):
        both = dot(rows, ref[...])
        gate, up = both[:, :units], both[:, units:]
        value = gate / (1.0 + jnp.exp(-gate)) * up
        held_ref[:, place * units : (place + 1) * units] = value.astype(BF)
    copies = [
        pltpu.make_async_copy(held_ref, out_ref.at[peer], done.at[peer])
        for peer in range(out_ref.shape[0])
    ]
    for copy in copies:
        copy.start()
    for copy in copies:
        copy.wait()


def hidden_units(rows, own, peer, peers):
    shape = (rows.shape[0], own.shape[1])
    return pl.pallas_call(
        hidden_kernel,
        out_shape=jax.ShapeDtypeStruct((peers, *shape), BF),
        in_specs=vmem(3),
        out_specs=hbm(),
        scratch_shapes=[pltpu.VMEM(shape, BF), pltpu.SemaphoreType.DMA((peers,))],
        compiler_params=PARAMS,
        name="hidden_units",
    )(rows, own, peer)


def down_kernel(yh_ref, h_ref, own_ref, peer_ref, out_ref):
    total = None
    count = h_ref.shape[0]
    for number in range(count):
        weights = jnp.concatenate([own_ref[number], peer_ref[number]], 0)
        term = dot(h_ref[(yh_ref[0] + count - number) % count], weights)
        total = term if total is None else total + term
    out_ref[...] = total.astype(BF)


def down(yh, h, own, peer):
    return pl.pallas_call(
        down_kernel,
        out_shape=jax.ShapeDtypeStruct((h.shape[1], own.shape[2]), BF),
        in_specs=[pl.BlockSpec(memory_space=pltpu.SMEM), *vmem(3)],
        out_specs=vmem(1)[0],
        compiler_params=PARAMS,
        name="down",
    )(yh.reshape(1), h, own, peer)


def combine_kernel(mix_ref, back_ref, out_ref, held_ref, done):
    peers, requests, _ = out_ref.shape
    rows = peers * requests
    value = dot(mix_ref[...], back_ref[...])
    value = (value[:rows] + value[rows:]).astype(BF)
    for peer in range(peers):
        held_ref[peer] = value[peer * requests : (peer + 1) * requests]
    copy = pltpu.make_async_copy(held_ref, out_ref, done)
    copy.start()
    copy.wait()


def combine(mix, back, requests):
    shape = (mix.shape[0] // 2 // requests, requests, back.shape[1])
    return pl.pallas_call(
        combine_kernel,
        out_shape=jax.ShapeDtypeStruct(shape, BF),
        in_specs=vmem(2),
        out_specs=hbm(),
        scratch_shapes=[pltpu.VMEM(shape, BF), pltpu.SemaphoreType.DMA],
        compiler_params=PARAMS,
        name="combine",
    )(mix, back)


def exchange(x, axes):
    return lax.all_to_all(x, axes, split_axis=0, concat_axis=0, tiled=True)


def shifted(x, axes, by):
    size = lax.axis_size(axes)
    return lax.ppermute(x, axes, [(i, (i + by) % size) for i in range(size)])


def shards(
    latent_cache,
    lengths,
    new_home,
    queries,
    new_latent,
    hidden,
    routes,
    route_logits,
    w_gate,
    w_up,
    w_down,
):
    experts = lax.axis_size(EP)
    yh_size, yl_size = lax.axis_size("yh"), lax.axis_size("yl")
    peers = experts // yl_size
    own_rank = lax.axis_index(EP)
    steps, _, requests, width = hidden.shape
    chunk = width // yh_size
    block = yl_size * CAP
    slots = peers * block

    packed = pack(hidden, routes, route_logits, yh_size * steps * yl_size)
    tokens = exchange(packed, COLUMN)
    served = attend(lengths[own_rank], queries, latent_cache, new_latent)
    tokens, served0, served1 = lax.optimization_barrier((tokens, *served))
    tokens = tokens.reshape(-1, tokens.shape[-1])
    send, mix = dispatch(lax.axis_index("yl"), tokens, slots, width)
    arrived = exchange(send.reshape(peers, block, width), PLANE).reshape(slots, width)

    own_w = jnp.concatenate([w_gate[0], w_up[0]], 1)
    peer_w = shifted(own_w, "c", 1)
    yh = lax.axis_index("yh")
    sent = [
        lax.dynamic_slice_in_dim(w_down[0], (yh + s) % yh_size * chunk, chunk, 1)
        for s in range(yh_size)
    ]
    own_down = jnp.stack([shifted(x, "yh", s) if s else x for s, x in enumerate(sent)])
    peer_down = shifted(own_down, "c", 1)

    far = shifted(served0, EP, experts // 2)
    arrived, peer_w, own_down, far = lax.optimization_barrier((arrived, peer_w, own_down, far))
    h = hidden_units(arrived, own_w, peer_w, yh_size)
    h, served1 = lax.optimization_barrier((h, served1))
    lower = shifted(served1, EP, 1)
    upper = shifted(served1, EP, -1)
    h, lower, upper = lax.optimization_barrier((exchange(h, "yh"), lower, upper))
    home = new_home[own_rank]
    result0 = jnp.where(home[0] == own_rank, served0, far)
    result1 = jnp.where(
        home[1] == own_rank,
        served1,
        jnp.where(home[1] == (own_rank + 1) % experts, upper, lower),
    )
    attended = jnp.stack([result0, result1], 1)[:, None]

    out = down(yh, h, own_down, peer_down)
    back = exchange(out.reshape(peers, block, chunk), PLANE).reshape(slots, chunk)
    final = exchange(combine(mix, back, requests), COLUMN)
    final = final.reshape(yh_size, steps, yl_size, requests, chunk).astype(F32)
    final = final.sum(2).astype(BF).transpose(1, 2, 0, 3)
    return attended, final.reshape(steps, 1, requests, width)


def solution(mesh):
    torus = Mesh(mesh.devices.reshape(4, 2, 2, 4, 8), ("yh", "c", "yl", "x", "z"))
    placed = (
        P(EP, DP, None, None),
        P(None, DP),
        P(None, DP),
        P(None, EP, DP, None, None),
        P(None, EP, DP, None),
        P(None, EP, DP, None),
        P(None, EP, DP, None),
        P(None, EP, DP, None),
        P(EP, None, DP),
        P(EP, None, DP),
        P(EP, DP, None),
    )
    return jax.shard_map(
        shards,
        mesh=torus,
        in_specs=placed,
        out_specs=(P(None, EP, DP, None, None), P(None, EP, DP, None)),
        check_vma=False,
    )
```

```python
import functools

import jax
import jax.numpy as jnp
from jax import lax
from jax.experimental import pallas as pl
from jax.experimental.pallas import tpu as pltpu
from jax.sharding import Mesh
from jax.sharding import PartitionSpec as P

KV_RANK = 512
HEAD_QK = 192
CAP = 4
EP = ("yl", "x", "z")
DP = ("yh", "c")
LINE = ("yh", "c", "z")
PLANE = ("yl", "x")
BF = jnp.bfloat16
F32 = jnp.float32
PARAMS = pltpu.CompilerParams(vmem_limit_bytes=48 * 1024 * 1024)


def dot(a, b, dims=((1,), (0,))):
    return lax.dot_general(a, b, (dims, ((), ())), preferred_element_type=F32)


def iota(shape, dim):
    return lax.broadcasted_iota(jnp.int32, shape, dim)


def vmem(n):
    return [pl.BlockSpec(memory_space=pltpu.VMEM)] * n


def attend_kernel(len_ref, query_ref, cache_ref, fresh_ref, out0_ref, out1_ref, keys_ref):
    steps, _, requests, heads, width = query_ref.shape
    cached = cache_ref.shape[2]
    total = keys_ref.shape[0]
    rows = steps * heads
    column = iota((rows, total), 1)
    row_step = iota((rows, total), 0) // heads
    for request, out_ref in zip(range(requests), (out0_ref, out1_ref)):
        keys_ref[:cached] = cache_ref[0, request]
        place = iota((total - cached, width), 0)
        tail = jnp.zeros((total - cached, width), F32)
        for step in range(steps):
            row = fresh_ref[step, 0, request : request + 1, :].astype(F32)
            tail = jnp.where(place == step, row, tail)
        keys_ref[cached:] = tail.astype(BF)
        query = query_ref[:, 0, request].reshape(rows, width)
        keys = keys_ref[...]
        scores = dot(query, keys, ((1,), (1,))) * (HEAD_QK**-0.5)
        old = column < len_ref[request]
        new = (column >= cached) & (column - cached <= row_step)
        scores = jnp.where(old | new, scores, -jnp.inf)
        weights = jnp.exp(scores - jnp.max(scores, 1, keepdims=True))
        probs = (weights / jnp.sum(weights, 1, keepdims=True)).astype(BF)
        served = dot(probs, keys[:, :KV_RANK]).astype(BF)
        out_ref[...] = served.reshape(steps, heads, KV_RANK)


def attend(length, queries, cache, fresh):
    steps, _, _, heads, width = queries.shape
    out = jax.ShapeDtypeStruct((steps, heads, KV_RANK), BF)
    return pl.pallas_call(
        attend_kernel,
        out_shape=(out, out),
        in_specs=[pl.BlockSpec(memory_space=pltpu.SMEM), *vmem(3)],
        out_specs=tuple(vmem(2)),
        scratch_shapes=[pltpu.VMEM((cache.shape[2] + 128, width), BF)],
        compiler_params=PARAMS,
        name="attend",
    )(length, queries, cache, fresh)


def hbm():
    return pl.BlockSpec(memory_space=pltpu.HBM)


def pack_kernel(inner, hidden_ref, routes_ref, logits_ref, out_ref, *scratch):
    hidden_now, routes_now, logits_now, rows_ref, done = scratch
    pairs = ((hidden_ref, hidden_now), (routes_ref, routes_now), (logits_ref, logits_now))
    loads = [
        pltpu.make_async_copy(source, target, done.at[number])
        for number, (source, target) in enumerate(pairs)
    ]
    for load in loads:
        load.start()
    for load in loads:
        load.wait()
    steps, _, _, width = hidden_ref.shape
    for step in range(steps):
        parts = (routes_now[step, 0].astype(F32), logits_now[step, 0].astype(F32))
        tail = jnp.concatenate(parts, -1).astype(BF)
        for place in range(inner):
            rows_ref[step * inner + place, :, :width] = hidden_now[step, 0]
            rows_ref[step * inner + place, :, width:] = tail
    size = steps * inner
    stores = [
        pltpu.make_async_copy(rows_ref, out_ref.at[pl.ds(first, size)], done.at[first // size])
        for first in range(0, out_ref.shape[0], size)
    ]
    for store in stores:
        store.start()
    for store in stores:
        store.wait()


def pack(hidden, routes, logits, outer, inner):
    steps, _, requests, width = hidden.shape
    block = (requests, width + routes.shape[3] + logits.shape[3])
    return pl.pallas_call(
        functools.partial(pack_kernel, inner),
        out_shape=jax.ShapeDtypeStruct((outer * steps * inner, *block), BF),
        in_specs=[hbm()] * 3,
        out_specs=hbm(),
        scratch_shapes=[
            pltpu.VMEM(hidden.shape, BF),
            pltpu.VMEM(routes.shape, routes.dtype),
            pltpu.VMEM(logits.shape, BF),
            pltpu.VMEM((steps * inner, *block), BF),
            pltpu.SemaphoreType.DMA((max(outer, 3),)),
        ],
        compiler_params=PARAMS,
        name="pack",
    )(hidden, routes, logits)


def chosen_slots(z, line, tail, slots):
    rows, top = tail.shape
    slot = iota((rows, slots), 1)
    expert = (slot // (CAP * line) * line + z).astype(F32)
    named = jnp.zeros((rows, slots), F32)
    for k in range(top):
        named = jnp.where(tail[:, k : k + 1] == expert, 1.0, named)
    this, other = iota((rows, rows), 0), iota((rows, rows), 1)
    before = ((other < this) & (other // 2 % line == this // 2 % line)).astype(F32)
    earlier = dot(before.astype(BF), named.astype(BF))
    chosen = (named > 0) & (earlier == (slot % CAP).astype(F32))
    return chosen & (slot // CAP % line == iota((rows, slots), 0) // 2 % line), expert


def dispatch_kernel(line, top, z_ref, tokens_ref, send_ref, held_ref, done):
    slots, width = send_ref.shape
    tail = tokens_ref[:, width : width + top].astype(F32)
    chosen, _ = chosen_slots(z_ref[0], line, tail, slots)
    pick = chosen.astype(F32).astype(BF)
    copies = []
    for part in range(0, slots, 128):
        span = slice(part, part + 128)
        sent = dot(pick[:, span], tokens_ref[:, :width], ((0,), (0,)))
        held_ref[span] = sent.astype(BF)
        copy = pltpu.make_async_copy(held_ref.at[span], send_ref.at[span], done.at[part // 128])
        copy.start()
        copies.append(copy)
    for copy in copies:
        copy.wait()


def dispatch(z, line, top, tokens, slots, width):
    return pl.pallas_call(
        functools.partial(dispatch_kernel, line, top),
        out_shape=jax.ShapeDtypeStruct((slots, width), BF),
        in_specs=[pl.BlockSpec(memory_space=pltpu.SMEM), *vmem(1)],
        out_specs=hbm(),
        scratch_shapes=[
            pltpu.VMEM((slots, width), BF),
            pltpu.SemaphoreType.DMA((slots // 128,)),
        ],
        compiler_params=PARAMS,
        name="dispatch",
    )(z, tokens)


def mix_kernel(line, z_ref, tail_ref, mix_ref):
    slots = mix_ref.shape[1]
    tail = tail_ref[...].astype(F32)
    top = tail.shape[1] // 2
    sigmoid = jax.nn.sigmoid(tail[:, top:])
    gates = 2.5 * sigmoid / jnp.sum(sigmoid, 1, keepdims=True)
    chosen, expert = chosen_slots(z_ref[0], line, tail[:, :top], slots)
    gate = jnp.zeros(chosen.shape, F32)
    for k in range(top):
        gate = jnp.where(tail[:, k : k + 1] == expert, gates[:, k : k + 1], gate)
    high = gate.astype(BF).astype(F32)
    mix = [jnp.where(chosen, part, 0.0) for part in (high, gate - high)]
    mix_ref[...] = jnp.concatenate(mix, 0).astype(BF)


def mixing(z, line, tail, slots):
    return pl.pallas_call(
        functools.partial(mix_kernel, line),
        out_shape=jax.ShapeDtypeStruct((2 * tail.shape[0], slots), BF),
        in_specs=[pl.BlockSpec(memory_space=pltpu.SMEM), *vmem(1)],
        out_specs=vmem(1)[0],
        compiler_params=PARAMS,
        name="mixing",
    )(z, tail)


def hidden_kernel(rows_ref, own_ref, peer_ref, out_ref, held_ref, done):
    units = own_ref.shape[1] // 2
    rows = rows_ref[...]
    copies = []
    for place, ref in enumerate((own_ref, peer_ref)):
        both = dot(rows, ref[...])
        gate, up = both[:, :units], both[:, units:]
        value = gate / (1.0 + jnp.exp(-gate)) * up
        held_ref[place] = value.astype(BF)
        for peer in range(out_ref.shape[0]):
            target = out_ref.at[peer, :, pl.ds(place * units, units)]
            copy = pltpu.make_async_copy(held_ref.at[place], target, done.at[place, peer])
            copy.start()
            copies.append(copy)
    for copy in copies:
        copy.wait()


def hidden_units(rows, own, peer, peers):
    shape = (rows.shape[0], own.shape[1])
    return pl.pallas_call(
        hidden_kernel,
        out_shape=jax.ShapeDtypeStruct((peers, *shape), BF),
        in_specs=vmem(3),
        out_specs=hbm(),
        scratch_shapes=[
            pltpu.VMEM((2, shape[0], shape[1] // 2), BF),
            pltpu.SemaphoreType.DMA((2, peers)),
        ],
        compiler_params=PARAMS,
        name="hidden_units",
    )(rows, own, peer)


def down_kernel(yh_ref, h_ref, own_ref, peer_ref, out_ref):
    total = None
    count = h_ref.shape[0]
    for number in range(count):
        weights = jnp.concatenate([own_ref[number], peer_ref[number]], 0)
        term = dot(h_ref[(yh_ref[0] + count - number) % count], weights)
        total = term if total is None else total + term
    out_ref[...] = total.astype(BF)


def down(yh, h, own, peer):
    return pl.pallas_call(
        down_kernel,
        out_shape=jax.ShapeDtypeStruct((h.shape[1], own.shape[2]), BF),
        in_specs=[pl.BlockSpec(memory_space=pltpu.SMEM), *vmem(3)],
        out_specs=vmem(1)[0],
        compiler_params=PARAMS,
        name="down",
    )(yh.reshape(1), h, own, peer)


def combine_kernel(mix_ref, back_ref, out_ref, held_ref, done):
    peers, requests, _ = out_ref.shape
    rows = peers * requests
    value = dot(mix_ref[...], back_ref[...])
    value = (value[:rows] + value[rows:]).astype(BF)
    for peer in range(peers):
        held_ref[peer] = value[peer * requests : (peer + 1) * requests]
    copy = pltpu.make_async_copy(held_ref, out_ref, done)
    copy.start()
    copy.wait()


def combine(mix, back, requests):
    shape = (mix.shape[0] // 2 // requests, requests, back.shape[1])
    return pl.pallas_call(
        combine_kernel,
        out_shape=jax.ShapeDtypeStruct(shape, BF),
        in_specs=vmem(2),
        out_specs=hbm(),
        scratch_shapes=[pltpu.VMEM(shape, BF), pltpu.SemaphoreType.DMA],
        compiler_params=PARAMS,
        name="combine",
    )(mix, back)


def exchange(x, axes):
    return lax.all_to_all(x, axes, split_axis=0, concat_axis=0, tiled=True)


def shifted(x, axes, by):
    size = lax.axis_size(axes)
    return lax.ppermute(x, axes, [(i, (i + by) % size) for i in range(size)])


def shards(
    latent_cache,
    lengths,
    new_home,
    queries,
    new_latent,
    hidden,
    routes,
    route_logits,
    w_gate,
    w_up,
    w_down,
):
    experts = lax.axis_size(EP)
    yh_size, line = lax.axis_size("yh"), lax.axis_size("z")
    peers = experts // line
    own_rank = lax.axis_index(EP)
    yh, z = lax.axis_index("yh"), lax.axis_index("z").reshape(1)
    steps, _, requests, width = hidden.shape
    top = routes.shape[3]
    chunk = width // yh_size
    slots = experts * CAP

    packed = pack(hidden, routes, route_logits, yh_size, line)
    tokens = exchange(packed, LINE)
    served = attend(lengths[own_rank], queries, latent_cache, new_latent)
    served, w_gate, w_up = lax.optimization_barrier((served, w_gate, w_up))
    own_w = jnp.concatenate([w_gate[0], w_up[0]], 1)
    peer_w = shifted(own_w, "c", 1)
    sent = [
        lax.dynamic_slice_in_dim(w_down[0], (yh + s) % yh_size * chunk, chunk, 1)
        for s in range(yh_size)
    ]
    moved = [shifted(x, "yh", s) if s in (1, yh_size - 1) else x for s, x in enumerate(sent)]
    tokens, peer_w, served0, served1, *moved = lax.optimization_barrier(
        (tokens, peer_w, *served, *moved)
    )
    tokens = tokens.reshape(-1, tokens.shape[-1])
    send = dispatch(z, line, top, tokens, slots, width)
    arrived = exchange(send.reshape(peers, -1, width), PLANE).reshape(slots, width)
    mix = mixing(z, line, tokens[:, width:], slots)
    moved = [shifted(x, "yh", s) if 1 < s < yh_size - 1 else x for s, x in enumerate(moved)]
    own_down = jnp.stack(moved)
    peer_down = shifted(own_down, "c", 1)

    far = shifted(served0, EP, experts // 2)
    arrived, peer_w, far, mix = lax.optimization_barrier((arrived, peer_w, far, mix))
    h = hidden_units(arrived, own_w, peer_w, yh_size)
    h, own_down = lax.optimization_barrier((h, own_down))
    h, served1 = lax.optimization_barrier((exchange(h, "yh"), served1))
    lower = shifted(served1, EP, 1)
    upper = shifted(served1, EP, -1)
    home = new_home[own_rank]
    result0 = jnp.where(home[0] == own_rank, served0, far)
    result1 = jnp.where(
        home[1] == own_rank,
        served1,
        jnp.where(home[1] == (own_rank + 1) % experts, upper, lower),
    )
    attended = jnp.stack([result0, result1], 1)[:, None]

    out = down(yh, h, own_down, peer_down)
    back = exchange(out.reshape(peers, -1, chunk), PLANE).reshape(slots, chunk)
    final = exchange(combine(mix, back, requests), LINE)
    final = final.reshape(yh_size, steps, line, requests, chunk).astype(F32)
    final = final.sum(2).astype(BF).transpose(1, 2, 0, 3)
    return attended, final.reshape(steps, 1, requests, width)


def solution(mesh):
    torus = Mesh(mesh.devices.reshape(4, 2, 2, 4, 8), ("yh", "c", "yl", "x", "z"))
    placed = (
        P(EP, DP, None, None),
        P(None, DP),
        P(None, DP),
        P(None, EP, DP, None, None),
        P(None, EP, DP, None),
        P(None, EP, DP, None),
        P(None, EP, DP, None),
        P(None, EP, DP, None),
        P(EP, None, DP),
        P(EP, None, DP),
        P(EP, DP, None),
    )
    return jax.shard_map(
        shards,
        mesh=torus,
        in_specs=placed,
        out_specs=(P(None, EP, DP, None, None), P(None, EP, DP, None)),
        check_vma=False,
    )
```

```python
import functools

import jax
import jax.numpy as jnp
from jax import lax
from jax.experimental import pallas as pl
from jax.experimental.pallas import tpu as pltpu
from jax.sharding import Mesh
from jax.sharding import PartitionSpec as P

KV_RANK = 512
HEAD_QK = 192
CAP = 4
EP = ("yl", "x", "z")
DP = ("yh", "c")
COLUMN = ("yh", "c", "yl")
PLANE = ("x", "z")
BF = jnp.bfloat16
F32 = jnp.float32
ALL_VMEM = pltpu.CompilerParams(vmem_limit_bytes=60 * 1024 * 1024)
PARAMS = pltpu.CompilerParams(vmem_limit_bytes=48 * 1024 * 1024)


def dot(a, b, dims=((1,), (0,))):
    return lax.dot_general(a, b, (dims, ((), ())), preferred_element_type=F32)


def iota(shape, dim):
    return lax.broadcasted_iota(jnp.int32, shape, dim)


def vmem(n):
    return [pl.BlockSpec(memory_space=pltpu.VMEM)] * n


def attend_kernel(len_ref, query_ref, cache_ref, fresh_ref, out0_ref, out1_ref, keys_ref):
    steps, _, requests, heads, width = query_ref.shape
    cached = cache_ref.shape[2]
    total = keys_ref.shape[0]
    rows = steps * heads
    column = iota((rows, total), 1)
    row_step = iota((rows, total), 0) // heads
    for request, out_ref in zip(range(requests), (out0_ref, out1_ref)):
        keys_ref[:cached] = cache_ref[0, request]
        place = iota((total - cached, width), 0)
        tail = jnp.zeros((total - cached, width), F32)
        for step in range(steps):
            row = fresh_ref[step, 0, request : request + 1, :].astype(F32)
            tail = jnp.where(place == step, row, tail)
        keys_ref[cached:] = tail.astype(BF)
        query = query_ref[:, 0, request].reshape(rows, width)
        keys = keys_ref[...]
        scores = dot(query, keys, ((1,), (1,))) * (HEAD_QK**-0.5)
        old = column < len_ref[request]
        new = (column >= cached) & (column - cached <= row_step)
        scores = jnp.where(old | new, scores, -jnp.inf)
        weights = jnp.exp(scores - jnp.max(scores, 1, keepdims=True))
        probs = (weights / jnp.sum(weights, 1, keepdims=True)).astype(BF)
        served = dot(probs, keys[:, :KV_RANK]).astype(BF)
        out_ref[...] = served.reshape(steps, heads, KV_RANK)


def attend(length, queries, cache, fresh):
    steps, _, _, heads, width = queries.shape
    out = jax.ShapeDtypeStruct((steps, heads, KV_RANK), BF)
    return pl.pallas_call(
        attend_kernel,
        out_shape=(out, out),
        in_specs=[pl.BlockSpec(memory_space=pltpu.SMEM), *vmem(3)],
        out_specs=tuple(vmem(2)),
        scratch_shapes=[pltpu.VMEM((cache.shape[2] + 128, width), BF)],
        compiler_params=PARAMS,
        name="attend",
    )(length, queries, cache, fresh)


def hbm():
    return pl.BlockSpec(memory_space=pltpu.HBM)


def pack_kernel(inner, hidden_ref, routes_ref, logits_ref, out_ref, *scratch):
    hidden_now, routes_now, logits_now, rows_ref, done = scratch
    pairs = ((hidden_ref, hidden_now), (routes_ref, routes_now), (logits_ref, logits_now))
    loads = [
        pltpu.make_async_copy(source, target, done.at[number])
        for number, (source, target) in enumerate(pairs)
    ]
    for load in loads:
        load.start()
    for load in loads:
        load.wait()
    steps, _, _, width = hidden_ref.shape
    for step in range(steps):
        parts = (routes_now[step, 0].astype(F32), logits_now[step, 0].astype(F32))
        tail = jnp.concatenate(parts, -1).astype(BF)
        for place in range(inner):
            rows_ref[step * inner + place, :, :width] = hidden_now[step, 0]
            rows_ref[step * inner + place, :, width:] = tail
    size = steps * inner
    stores = [
        pltpu.make_async_copy(rows_ref, out_ref.at[pl.ds(first, size)], done.at[first // size])
        for first in range(0, out_ref.shape[0], size)
    ]
    for store in stores:
        store.start()
    for store in stores:
        store.wait()


def pack(hidden, routes, logits, outer, inner):
    steps, _, requests, width = hidden.shape
    block = (requests, width + routes.shape[3] + logits.shape[3])
    return pl.pallas_call(
        functools.partial(pack_kernel, inner),
        out_shape=jax.ShapeDtypeStruct((outer * steps * inner, *block), BF),
        in_specs=[hbm()] * 3,
        out_specs=hbm(),
        scratch_shapes=[
            pltpu.VMEM(hidden.shape, BF),
            pltpu.VMEM(routes.shape, routes.dtype),
            pltpu.VMEM(logits.shape, BF),
            pltpu.VMEM((steps * inner, *block), BF),
            pltpu.SemaphoreType.DMA((max(outer, 3),)),
        ],
        compiler_params=ALL_VMEM,
        name="pack",
    )(hidden, routes, logits)


def chosen_slots(yl, tail, slots):
    rows, top = tail.shape
    slot = iota((rows, slots), 1)
    expert = (slot // (2 * CAP) + yl * (slots // (2 * CAP))).astype(F32)
    named = jnp.zeros((rows, slots), F32)
    for k in range(top):
        named = jnp.where(tail[:, k : k + 1] == expert, 1.0, named)
    this, other = iota((rows, rows), 0), iota((rows, rows), 1)
    before = ((other < this) & (other // 2 % 2 == this // 2 % 2)).astype(F32)
    earlier = dot(before.astype(BF), named.astype(BF))
    chosen = (named > 0) & (earlier == (slot % CAP).astype(F32))
    return chosen & (slot % (2 * CAP) // CAP == iota((rows, slots), 0) // 2 % 2), expert


def dispatch_kernel(top, yl_ref, tokens_ref, send_ref, held_ref, done):
    peers, block, width = send_ref.shape
    tail = tokens_ref[:, width : width + top].astype(F32)
    chosen, _ = chosen_slots(yl_ref[0], tail, peers * block)
    pick = chosen.astype(F32).astype(BF)
    copies = []
    group = 128 // block
    for part in range(peers // group):
        span = pl.ds(part * group, group)
        lanes = slice(part * 128, (part + 1) * 128)
        sent = dot(pick[:, lanes], tokens_ref[:, :width], ((0,), (0,)))
        held_ref[span] = sent.reshape(group, block, width).astype(BF)
        copy = pltpu.make_async_copy(held_ref.at[span], send_ref.at[span], done.at[part])
        copy.start()
        copies.append(copy)
    for copy in copies:
        copy.wait()


def dispatch(yl, top, tokens, peers, block, width):
    return pl.pallas_call(
        functools.partial(dispatch_kernel, top),
        out_shape=jax.ShapeDtypeStruct((peers, block, width), BF),
        in_specs=[pl.BlockSpec(memory_space=pltpu.SMEM), *vmem(1)],
        out_specs=hbm(),
        scratch_shapes=[
            pltpu.VMEM((peers, block, width), BF),
            pltpu.SemaphoreType.DMA((peers * block // 128,)),
        ],
        compiler_params=PARAMS,
        name="dispatch",
    )(yl, tokens)


def mix_kernel(yl_ref, tail_ref, mix_ref):
    slots = mix_ref.shape[1]
    tail = tail_ref[...].astype(F32)
    top = tail.shape[1] // 2
    sigmoid = jax.nn.sigmoid(tail[:, top:])
    gates = 2.5 * sigmoid / jnp.sum(sigmoid, 1, keepdims=True)
    chosen, expert = chosen_slots(yl_ref[0], tail[:, :top], slots)
    gate = jnp.zeros(chosen.shape, F32)
    for k in range(top):
        gate = jnp.where(tail[:, k : k + 1] == expert, gates[:, k : k + 1], gate)
    high = gate.astype(BF).astype(F32)
    mix = [jnp.where(chosen, part, 0.0) for part in (high, gate - high)]
    mix_ref[...] = jnp.concatenate(mix, 0).astype(BF)


def mixing(yl, tail, slots):
    return pl.pallas_call(
        mix_kernel,
        out_shape=jax.ShapeDtypeStruct((2 * tail.shape[0], slots), BF),
        in_specs=[pl.BlockSpec(memory_space=pltpu.SMEM), *vmem(1)],
        out_specs=vmem(1)[0],
        compiler_params=PARAMS,
        name="mixing",
    )(yl, tail)


def hidden_kernel(rows_ref, own_ref, peer_ref, out_ref, held_ref, done):
    units = own_ref.shape[1] // 2
    rows = rows_ref[...]
    for place, ref in enumerate((own_ref, peer_ref)):
        both = dot(rows, ref[...])
        gate, up = both[:, :units], both[:, units:]
        value = gate / (1.0 + jnp.exp(-gate)) * up
        held_ref[:, place * units : (place + 1) * units] = value.astype(BF)
    copies = [
        pltpu.make_async_copy(held_ref, out_ref.at[peer], done.at[peer])
        for peer in range(out_ref.shape[0])
    ]
    for copy in copies:
        copy.start()
    for copy in copies:
        copy.wait()


def hidden_units(rows, own, peer, peers):
    shape = (rows.shape[0], own.shape[1])
    return pl.pallas_call(
        hidden_kernel,
        out_shape=jax.ShapeDtypeStruct((peers, *shape), BF),
        in_specs=vmem(3),
        out_specs=hbm(),
        scratch_shapes=[pltpu.VMEM(shape, BF), pltpu.SemaphoreType.DMA((peers,))],
        compiler_params=PARAMS,
        name="hidden_units",
    )(rows, own, peer)


def down_kernel(yh_ref, h_ref, own_ref, peer_ref, out_ref):
    total = None
    count = h_ref.shape[0]
    for number in range(count):
        weights = jnp.concatenate([own_ref[number], peer_ref[number]], 0)
        term = dot(h_ref[(yh_ref[0] + count - number) % count], weights)
        total = term if total is None else total + term
    out_ref[...] = total.astype(BF)


def down(yh, h, own, peer):
    return pl.pallas_call(
        down_kernel,
        out_shape=jax.ShapeDtypeStruct((h.shape[1], own.shape[2]), BF),
        in_specs=[pl.BlockSpec(memory_space=pltpu.SMEM), *vmem(3)],
        out_specs=vmem(1)[0],
        compiler_params=PARAMS,
        name="down",
    )(yh.reshape(1), h, own, peer)


def combine_kernel(mix_ref, back_ref, out_ref, held_ref, done):
    peers, requests, _ = out_ref.shape
    rows = peers * requests
    value = dot(mix_ref[...], back_ref[...])
    value = (value[:rows] + value[rows:]).astype(BF)
    for peer in range(peers):
        held_ref[peer] = value[peer * requests : (peer + 1) * requests]
    copy = pltpu.make_async_copy(held_ref, out_ref, done)
    copy.start()
    copy.wait()


def combine(mix, back, requests):
    shape = (mix.shape[0] // 2 // requests, requests, back.shape[1])
    return pl.pallas_call(
        combine_kernel,
        out_shape=jax.ShapeDtypeStruct(shape, BF),
        in_specs=vmem(2),
        out_specs=hbm(),
        scratch_shapes=[pltpu.VMEM(shape, BF), pltpu.SemaphoreType.DMA],
        compiler_params=PARAMS,
        name="combine",
    )(mix, back)


def exchange(x, axes):
    return lax.all_to_all(x, axes, split_axis=0, concat_axis=0, tiled=True)


def shifted(x, axes, by):
    size = lax.axis_size(axes)
    return lax.ppermute(x, axes, [(i, (i + by) % size) for i in range(size)])


def shards(
    latent_cache,
    lengths,
    new_home,
    queries,
    new_latent,
    hidden,
    routes,
    route_logits,
    w_gate,
    w_up,
    w_down,
):
    experts = lax.axis_size(EP)
    yh_size, yl_size = lax.axis_size("yh"), lax.axis_size("yl")
    peers = experts // yl_size
    own_rank = lax.axis_index(EP)
    steps, _, requests, width = hidden.shape
    chunk = width // yh_size
    block = yl_size * CAP
    slots = peers * block

    top = routes.shape[3]
    yl = lax.axis_index("yl").reshape(1)

    packed = pack(hidden, routes, route_logits, yh_size, yl_size)
    tokens = exchange(packed, COLUMN)
    own_w = jnp.concatenate([w_gate[0], w_up[0]], 1)
    served = attend(lengths[own_rank], queries, latent_cache, new_latent)
    tokens, own_w, served0, served1 = lax.optimization_barrier((tokens, own_w, *served))
    tokens = tokens.reshape(-1, tokens.shape[-1])
    send = dispatch(yl, top, tokens, peers, block, width)
    arrived = exchange(send, PLANE).reshape(slots, width)

    far = shifted(served0, EP, experts // 2)
    lower = shifted(served1, EP, 1)
    upper = shifted(served1, EP, -1)
    mix = mixing(yl, tokens[:, width:], slots)
    peer_w = shifted(own_w, "c", 1)
    yh = lax.axis_index("yh")
    sent = [
        lax.dynamic_slice_in_dim(w_down[0], (yh + s) % yh_size * chunk, chunk, 1)
        for s in range(yh_size)
    ]
    own_down = jnp.stack([shifted(x, "yh", s) if s else x for s, x in enumerate(sent)])
    peer_down = shifted(own_down, "c", 1)
    arrived, peer_w, own_down, mix, far, lower, upper = lax.optimization_barrier(
        (arrived, peer_w, own_down, mix, far, lower, upper)
    )
    h = exchange(hidden_units(arrived, own_w, peer_w, yh_size), "yh")
    home = new_home[own_rank]
    result0 = jnp.where(home[0] == own_rank, served0, far)
    result1 = jnp.where(
        home[1] == own_rank,
        served1,
        jnp.where(home[1] == (own_rank + 1) % experts, upper, lower),
    )
    attended = jnp.stack([result0, result1], 1)[:, None]

    out = down(yh, h, own_down, peer_down)
    back = exchange(out.reshape(peers, block, chunk), PLANE).reshape(slots, chunk)
    final = exchange(combine(mix, back, requests), COLUMN)
    final = final.reshape(yh_size, steps, yl_size, requests, chunk).astype(F32)
    final = final.sum(2).astype(BF).transpose(1, 2, 0, 3)
    return attended, final.reshape(steps, 1, requests, width)


def solution(mesh):
    torus = Mesh(mesh.devices.reshape(4, 2, 2, 4, 8), ("yh", "c", "yl", "x", "z"))
    placed = (
        P(EP, DP, None, None),
        P(None, DP),
        P(None, DP),
        P(None, EP, DP, None, None),
        P(None, EP, DP, None),
        P(None, EP, DP, None),
        P(None, EP, DP, None),
        P(None, EP, DP, None),
        P(EP, None, DP),
        P(EP, None, DP),
        P(EP, DP, None),
    )
    return jax.shard_map(
        shards,
        mesh=torus,
        in_specs=placed,
        out_specs=(P(None, EP, DP, None, None), P(None, EP, DP, None)),
        check_vma=False,
    )
```

```python
import functools

import jax
import jax.numpy as jnp
from jax import lax
from jax.experimental import pallas as pl
from jax.experimental.pallas import tpu as pltpu
from jax.sharding import Mesh
from jax.sharding import PartitionSpec as P

KV_RANK = 512
HEAD_QK = 192
CAP = 4
EP = ("yl", "x", "z")
DP = ("yh", "c")
LINE = ("z", "yh", "c")
PLANE = ("yl", "x")
BF = jnp.bfloat16
F32 = jnp.float32
ALL_VMEM = pltpu.CompilerParams(vmem_limit_bytes=60 * 1024 * 1024)
PARAMS = pltpu.CompilerParams(vmem_limit_bytes=48 * 1024 * 1024)


def dot(a, b, dims=((1,), (0,))):
    return lax.dot_general(a, b, (dims, ((), ())), preferred_element_type=F32)


def iota(shape, dim):
    return lax.broadcasted_iota(jnp.int32, shape, dim)


def vmem(n):
    return [pl.BlockSpec(memory_space=pltpu.VMEM)] * n


def attend_kernel(len_ref, query_ref, cache_ref, fresh_ref, out0_ref, out1_ref, keys_ref):
    steps, _, requests, heads, width = query_ref.shape
    cached = cache_ref.shape[2]
    total = keys_ref.shape[0]
    rows = steps * heads
    column = iota((rows, total), 1)
    row_step = iota((rows, total), 0) // heads
    for request, out_ref in zip(range(requests), (out0_ref, out1_ref)):
        keys_ref[:cached] = cache_ref[0, request]
        place = iota((total - cached, width), 0)
        tail = jnp.zeros((total - cached, width), F32)
        for step in range(steps):
            row = fresh_ref[step, 0, request : request + 1, :].astype(F32)
            tail = jnp.where(place == step, row, tail)
        keys_ref[cached:] = tail.astype(BF)
        query = query_ref[:, 0, request].reshape(rows, width)
        keys = keys_ref[...]
        scores = dot(query, keys, ((1,), (1,))) * (HEAD_QK**-0.5)
        old = column < len_ref[request]
        new = (column >= cached) & (column - cached <= row_step)
        scores = jnp.where(old | new, scores, -jnp.inf)
        weights = jnp.exp(scores - jnp.max(scores, 1, keepdims=True))
        probs = (weights / jnp.sum(weights, 1, keepdims=True)).astype(BF)
        served = dot(probs, keys[:, :KV_RANK]).astype(BF)
        out_ref[...] = served.reshape(steps, heads, KV_RANK)


def attend(length, queries, cache, fresh):
    steps, _, _, heads, width = queries.shape
    out = jax.ShapeDtypeStruct((steps, heads, KV_RANK), BF)
    return pl.pallas_call(
        attend_kernel,
        out_shape=(out, out),
        in_specs=[pl.BlockSpec(memory_space=pltpu.SMEM), *vmem(3)],
        out_specs=tuple(vmem(2)),
        scratch_shapes=[pltpu.VMEM((cache.shape[2] + 128, width), BF)],
        compiler_params=PARAMS,
        name="attend",
    )(length, queries, cache, fresh)


def hbm():
    return pl.BlockSpec(memory_space=pltpu.HBM)


def pack_kernel(inner, hidden_ref, routes_ref, logits_ref, out_ref, *scratch):
    hidden_now, routes_now, logits_now, rows_ref, done = scratch
    pairs = ((hidden_ref, hidden_now), (routes_ref, routes_now), (logits_ref, logits_now))
    loads = [
        pltpu.make_async_copy(source, target, done.at[number])
        for number, (source, target) in enumerate(pairs)
    ]
    for load in loads:
        load.start()
    for load in loads:
        load.wait()
    steps, _, _, width = hidden_ref.shape
    for step in range(steps):
        parts = (routes_now[step, 0].astype(F32), logits_now[step, 0].astype(F32))
        tail = jnp.concatenate(parts, -1).astype(BF)
        for place in range(inner):
            rows_ref[step * inner + place, :, :width] = hidden_now[step, 0]
            rows_ref[step * inner + place, :, width:] = tail
    size = steps * inner
    stores = [
        pltpu.make_async_copy(rows_ref, out_ref.at[pl.ds(first, size)], done.at[first // size])
        for first in range(0, out_ref.shape[0], size)
    ]
    for store in stores:
        store.start()
    for store in stores:
        store.wait()


def pack(hidden, routes, logits, outer, inner):
    steps, _, requests, width = hidden.shape
    block = (requests, width + routes.shape[3] + logits.shape[3])
    return pl.pallas_call(
        functools.partial(pack_kernel, inner),
        out_shape=jax.ShapeDtypeStruct((outer * steps * inner, *block), BF),
        in_specs=[hbm()] * 3,
        out_specs=hbm(),
        scratch_shapes=[
            pltpu.VMEM(hidden.shape, BF),
            pltpu.VMEM(routes.shape, routes.dtype),
            pltpu.VMEM(logits.shape, BF),
            pltpu.VMEM((steps * inner, *block), BF),
            pltpu.SemaphoreType.DMA((max(outer, 3),)),
        ],
        compiler_params=ALL_VMEM,
        name="pack",
    )(hidden, routes, logits)


def chosen_slots(z, line, tail, slots):
    rows, top = tail.shape
    slot = iota((rows, slots), 1)
    expert = (slot // (CAP * line) * line + z).astype(F32)
    named = jnp.zeros((rows, slots), F32)
    for k in range(top):
        named = jnp.where(tail[:, k : k + 1] == expert, 1.0, named)
    this, other = iota((rows, rows), 0), iota((rows, rows), 1)
    group = rows // line
    before = ((other < this) & (other // group == this // group)).astype(F32)
    earlier = dot(before.astype(BF), named.astype(BF))
    chosen = (named > 0) & (earlier == (slot % CAP).astype(F32))
    return chosen & (slot // CAP % line == iota((rows, slots), 0) // group), expert


def spread_kernel(tokens_ref, out_ref, held_ref, done):
    blocks, requests, _ = tokens_ref.shape
    for block in range(blocks):
        held_ref[block * requests : (block + 1) * requests] = tokens_ref[block]
    copies = [
        pltpu.make_async_copy(held_ref, out_ref.at[peer], done.at[peer])
        for peer in range(out_ref.shape[0])
    ]
    for copy in copies:
        copy.start()
    for copy in copies:
        copy.wait()


def spread(tokens, peers):
    shape = (tokens.shape[0] * tokens.shape[1], tokens.shape[2])
    return pl.pallas_call(
        spread_kernel,
        out_shape=jax.ShapeDtypeStruct((peers, *shape), BF),
        in_specs=vmem(1),
        out_specs=hbm(),
        scratch_shapes=[pltpu.VMEM(shape, BF), pltpu.SemaphoreType.DMA((peers,))],
        compiler_params=PARAMS,
        name="spread",
    )(tokens)


def dispatch_kernel(line, top, z_ref, tokens_ref, send_ref, held_ref, done):
    peers, block, width = send_ref.shape
    tail = tokens_ref[:, width : width + top].astype(F32)
    chosen, _ = chosen_slots(z_ref[0], line, tail, peers * block)
    pick = chosen.astype(F32).astype(BF)
    copies = []
    group = 128 // block
    for part in range(peers // group):
        span = pl.ds(part * group, group)
        lanes = slice(part * 128, (part + 1) * 128)
        sent = dot(pick[:, lanes], tokens_ref[:, :width], ((0,), (0,)))
        held_ref[span] = sent.reshape(group, block, width).astype(BF)
        copy = pltpu.make_async_copy(held_ref.at[span], send_ref.at[span], done.at[part])
        copy.start()
        copies.append(copy)
    for copy in copies:
        copy.wait()


def dispatch(z, line, top, tokens, peers, block, width):
    return pl.pallas_call(
        functools.partial(dispatch_kernel, line, top),
        out_shape=jax.ShapeDtypeStruct((peers, block, width), BF),
        in_specs=[pl.BlockSpec(memory_space=pltpu.SMEM), *vmem(1)],
        out_specs=hbm(),
        scratch_shapes=[
            pltpu.VMEM((peers, block, width), BF),
            pltpu.SemaphoreType.DMA((peers * block // 128,)),
        ],
        compiler_params=PARAMS,
        name="dispatch",
    )(z, tokens)


def mix_kernel(line, z_ref, tail_ref, mix_ref):
    slots = mix_ref.shape[1]
    tail = tail_ref[...].astype(F32)
    top = tail.shape[1] // 2
    sigmoid = jax.nn.sigmoid(tail[:, top:])
    gates = 2.5 * sigmoid / jnp.sum(sigmoid, 1, keepdims=True)
    chosen, expert = chosen_slots(z_ref[0], line, tail[:, :top], slots)
    gate = jnp.zeros(chosen.shape, F32)
    for k in range(top):
        gate = jnp.where(tail[:, k : k + 1] == expert, gates[:, k : k + 1], gate)
    high = gate.astype(BF).astype(F32)
    mix = [jnp.where(chosen, part, 0.0) for part in (high, gate - high)]
    mix_ref[...] = jnp.concatenate(mix, 0).astype(BF)


def mixing(z, line, tail, slots):
    return pl.pallas_call(
        functools.partial(mix_kernel, line),
        out_shape=jax.ShapeDtypeStruct((2 * tail.shape[0], slots), BF),
        in_specs=[pl.BlockSpec(memory_space=pltpu.SMEM), *vmem(1)],
        out_specs=vmem(1)[0],
        compiler_params=PARAMS,
        name="mixing",
    )(z, tail)


def hidden_kernel(rows_ref, own_ref, peer_ref, out_ref, held_ref, done):
    units = own_ref.shape[1] // 2
    rows = rows_ref[...]
    for place, ref in enumerate((own_ref, peer_ref)):
        both = dot(rows, ref[...])
        gate, up = both[:, :units], both[:, units:]
        value = gate / (1.0 + jnp.exp(-gate)) * up
        held_ref[:, place * units : (place + 1) * units] = value.astype(BF)
    copies = [
        pltpu.make_async_copy(held_ref, out_ref.at[peer], done.at[peer])
        for peer in range(out_ref.shape[0])
    ]
    for copy in copies:
        copy.start()
    for copy in copies:
        copy.wait()


def hidden_units(rows, own, peer, peers):
    shape = (rows.shape[0], own.shape[1])
    return pl.pallas_call(
        hidden_kernel,
        out_shape=jax.ShapeDtypeStruct((peers, *shape), BF),
        in_specs=vmem(3),
        out_specs=hbm(),
        scratch_shapes=[pltpu.VMEM(shape, BF), pltpu.SemaphoreType.DMA((peers,))],
        compiler_params=PARAMS,
        name="hidden_units",
    )(rows, own, peer)


def down_kernel(yh_ref, h_ref, own_ref, peer_ref, out_ref):
    total = None
    count = h_ref.shape[0]
    for number in range(count):
        weights = jnp.concatenate([own_ref[number], peer_ref[number]], 0)
        term = dot(h_ref[(yh_ref[0] + count - number) % count], weights)
        total = term if total is None else total + term
    out_ref[...] = total.astype(BF)


def down(yh, h, own, peer):
    return pl.pallas_call(
        down_kernel,
        out_shape=jax.ShapeDtypeStruct((h.shape[1], own.shape[2]), BF),
        in_specs=[pl.BlockSpec(memory_space=pltpu.SMEM), *vmem(3)],
        out_specs=vmem(1)[0],
        compiler_params=PARAMS,
        name="down",
    )(yh.reshape(1), h, own, peer)


def combine_kernel(mix_ref, back_ref, out_ref, held_ref, done):
    peers, requests, _ = out_ref.shape
    rows = peers * requests
    value = dot(mix_ref[...], back_ref[...])
    value = (value[:rows] + value[rows:]).astype(BF)
    for peer in range(peers):
        held_ref[peer] = value[peer * requests : (peer + 1) * requests]
    copy = pltpu.make_async_copy(held_ref, out_ref, done)
    copy.start()
    copy.wait()


def combine(mix, back, requests):
    shape = (mix.shape[0] // 2 // requests, requests, back.shape[1])
    return pl.pallas_call(
        combine_kernel,
        out_shape=jax.ShapeDtypeStruct(shape, BF),
        in_specs=vmem(2),
        out_specs=hbm(),
        scratch_shapes=[pltpu.VMEM(shape, BF), pltpu.SemaphoreType.DMA],
        compiler_params=PARAMS,
        name="combine",
    )(mix, back)


def exchange(x, axes):
    return lax.all_to_all(x, axes, split_axis=0, concat_axis=0, tiled=True)


def shifted(x, axes, by):
    size = lax.axis_size(axes)
    return lax.ppermute(x, axes, [(i, (i + by) % size) for i in range(size)])


def shards(
    latent_cache,
    lengths,
    new_home,
    queries,
    new_latent,
    hidden,
    routes,
    route_logits,
    w_gate,
    w_up,
    w_down,
):
    experts = lax.axis_size(EP)
    yh_size, line = lax.axis_size("yh"), lax.axis_size("z")
    peers = experts // line
    own_rank = lax.axis_index(EP)
    yh, z = lax.axis_index("yh"), lax.axis_index("z").reshape(1)
    steps, _, requests, width = hidden.shape
    top = routes.shape[3]
    chunk = width // yh_size
    slots = experts * CAP

    block = slots // peers

    tokens = exchange(pack(hidden, routes, route_logits, yh_size, 1), DP)
    own_w = jnp.concatenate([w_gate[0], w_up[0]], 1)
    served = attend(lengths[own_rank], queries, latent_cache, new_latent)
    tokens, own_w, w_down, served0, served1 = lax.optimization_barrier(
        (tokens, own_w, w_down, *served)
    )
    tokens, own_w, w_down = lax.optimization_barrier((spread(tokens, line), own_w, w_down))
    tokens = exchange(tokens, "z").reshape(-1, width + 2 * top)

    def columns(by):
        return lax.dynamic_slice_in_dim(w_down[0], (yh + by) % yh_size * chunk, chunk, 1)

    peer_w = shifted(own_w, "c", 1)
    middle = yh_size // 2
    across = shifted(columns(middle), "yh", middle)
    far = shifted(served0, EP, experts // 2)
    tokens, peer_w, across, far, w_down, served1 = lax.optimization_barrier(
        (tokens, peer_w, across, far, w_down, served1)
    )
    send = dispatch(z, line, top, tokens, peers, block, width)
    arrived = exchange(send, PLANE).reshape(slots, width)

    lower = shifted(served1, EP, 1)
    upper = shifted(served1, EP, -1)
    moved = [columns(0), *(shifted(columns(s), "yh", s) for s in range(1, yh_size) if s != middle)]
    moved.insert(middle, across)
    own_down = jnp.stack(moved)
    mix = mixing(z, line, tokens[:, width:], slots)
    arrived, own_down, mix, lower, upper = lax.optimization_barrier(
        (arrived, own_down, mix, lower, upper)
    )
    h = hidden_units(arrived, own_w, peer_w, yh_size)
    h, own_down = lax.optimization_barrier((h, own_down))
    peer_down = shifted(own_down, "c", 1)
    h = exchange(h, "yh")
    home = new_home[own_rank]
    result0 = jnp.where(home[0] == own_rank, served0, far)
    result1 = jnp.where(
        home[1] == own_rank,
        served1,
        jnp.where(home[1] == (own_rank + 1) % experts, upper, lower),
    )
    attended = jnp.stack([result0, result1], 1)[:, None]

    out = down(yh, h, own_down, peer_down)
    back = exchange(out.reshape(peers, -1, chunk), PLANE).reshape(slots, chunk)
    final = exchange(combine(mix, back, requests), LINE)
    final = final.reshape(line, yh_size, steps, requests, chunk).astype(F32)
    final = final.sum(0).astype(BF).transpose(1, 2, 0, 3)
    return attended, final.reshape(steps, 1, requests, width)


def solution(mesh):
    torus = Mesh(mesh.devices.reshape(4, 2, 2, 4, 8), ("yh", "c", "yl", "x", "z"))
    placed = (
        P(EP, DP, None, None),
        P(None, DP),
        P(None, DP),
        P(None, EP, DP, None, None),
        P(None, EP, DP, None),
        P(None, EP, DP, None),
        P(None, EP, DP, None),
        P(None, EP, DP, None),
        P(EP, None, DP),
        P(EP, None, DP),
        P(EP, DP, None),
    )
    return jax.shard_map(
        shards,
        mesh=torus,
        in_specs=placed,
        out_specs=(P(None, EP, DP, None, None), P(None, EP, DP, None)),
        check_vma=False,
    )
```

```python
import functools

import jax
import jax.numpy as jnp
from jax import lax
from jax.experimental import pallas as pl
from jax.experimental.pallas import tpu as pltpu
from jax.sharding import Mesh
from jax.sharding import PartitionSpec as P

KV_RANK = 512
HEAD_QK = 192
CAP = 4
EP = ("yl", "x", "z")
DP = ("yh", "c")
COLUMN = ("yh", "c", "yl")
PLANE = ("x", "z")
BF = jnp.bfloat16
F32 = jnp.float32
ALL_VMEM = pltpu.CompilerParams(vmem_limit_bytes=60 * 1024 * 1024)
PARAMS = pltpu.CompilerParams(vmem_limit_bytes=48 * 1024 * 1024)


def dot(a, b, dims=((1,), (0,))):
    return lax.dot_general(a, b, (dims, ((), ())), preferred_element_type=F32)


def iota(shape, dim):
    return lax.broadcasted_iota(jnp.int32, shape, dim)


def vmem(n):
    return [pl.BlockSpec(memory_space=pltpu.VMEM)] * n


def attend_kernel(len_ref, query_ref, cache_ref, fresh_ref, out0_ref, out1_ref, keys_ref):
    steps, _, requests, heads, width = query_ref.shape
    cached = cache_ref.shape[2]
    total = keys_ref.shape[0]
    rows = steps * heads
    column = iota((rows, total), 1)
    row_step = iota((rows, total), 0) // heads
    for request, out_ref in zip(range(requests), (out0_ref, out1_ref)):
        keys_ref[:cached] = cache_ref[0, request]
        place = iota((total - cached, width), 0)
        tail = jnp.zeros((total - cached, width), F32)
        for step in range(steps):
            row = fresh_ref[step, 0, request : request + 1, :].astype(F32)
            tail = jnp.where(place == step, row, tail)
        keys_ref[cached:] = tail.astype(BF)
        query = query_ref[:, 0, request].reshape(rows, width)
        keys = keys_ref[...]
        scores = dot(query, keys, ((1,), (1,))) * (HEAD_QK**-0.5)
        old = column < len_ref[request]
        new = (column >= cached) & (column - cached <= row_step)
        scores = jnp.where(old | new, scores, -jnp.inf)
        weights = jnp.exp(scores - jnp.max(scores, 1, keepdims=True))
        probs = (weights / jnp.sum(weights, 1, keepdims=True)).astype(BF)
        served = dot(probs, keys[:, :KV_RANK]).astype(BF)
        out_ref[...] = served.reshape(steps, heads, KV_RANK)


def attend(length, queries, cache, fresh):
    steps, _, _, heads, width = queries.shape
    out = jax.ShapeDtypeStruct((steps, heads, KV_RANK), BF)
    return pl.pallas_call(
        attend_kernel,
        out_shape=(out, out),
        in_specs=[pl.BlockSpec(memory_space=pltpu.SMEM), *vmem(3)],
        out_specs=tuple(vmem(2)),
        scratch_shapes=[pltpu.VMEM((cache.shape[2] + 128, width), BF)],
        compiler_params=PARAMS,
        name="attend",
    )(length, queries, cache, fresh)


def hbm():
    return pl.BlockSpec(memory_space=pltpu.HBM)


def pack_kernel(inner, hidden_ref, routes_ref, logits_ref, out_ref, *scratch):
    hidden_now, routes_now, logits_now, rows_ref, done = scratch
    pairs = ((hidden_ref, hidden_now), (routes_ref, routes_now), (logits_ref, logits_now))
    loads = [
        pltpu.make_async_copy(source, target, done.at[number])
        for number, (source, target) in enumerate(pairs)
    ]
    for load in loads:
        load.start()
    for load in loads:
        load.wait()
    steps, _, _, width = hidden_ref.shape
    for step in range(steps):
        parts = (routes_now[step, 0].astype(F32), logits_now[step, 0].astype(F32))
        tail = jnp.concatenate(parts, -1).astype(BF)
        for place in range(inner):
            rows_ref[step * inner + place, :, :width] = hidden_now[step, 0]
            rows_ref[step * inner + place, :, width:] = tail
    size = steps * inner
    stores = [
        pltpu.make_async_copy(rows_ref, out_ref.at[pl.ds(first, size)], done.at[first // size])
        for first in range(0, out_ref.shape[0], size)
    ]
    for store in stores:
        store.start()
    for store in stores:
        store.wait()


def pack(hidden, routes, logits, outer, inner):
    steps, _, requests, width = hidden.shape
    block = (requests, width + routes.shape[3] + logits.shape[3])
    return pl.pallas_call(
        functools.partial(pack_kernel, inner),
        out_shape=jax.ShapeDtypeStruct((outer * steps * inner, *block), BF),
        in_specs=[hbm()] * 3,
        out_specs=hbm(),
        scratch_shapes=[
            pltpu.VMEM(hidden.shape, BF),
            pltpu.VMEM(routes.shape, routes.dtype),
            pltpu.VMEM(logits.shape, BF),
            pltpu.VMEM((steps * inner, *block), BF),
            pltpu.SemaphoreType.DMA((max(outer, 3),)),
        ],
        compiler_params=ALL_VMEM,
        name="pack",
    )(hidden, routes, logits)


def chosen_slots(yl, tail, slots):
    rows, top = tail.shape
    slot = iota((rows, slots), 1)
    expert = (slot // (2 * CAP) + yl * (slots // (2 * CAP))).astype(F32)
    named = jnp.zeros((rows, slots), F32)
    for k in range(top):
        named = jnp.where(tail[:, k : k + 1] == expert, 1.0, named)
    this, other = iota((rows, rows), 0), iota((rows, rows), 1)
    before = ((other < this) & (other // 2 % 2 == this // 2 % 2)).astype(F32)
    earlier = dot(before.astype(BF), named.astype(BF))
    chosen = (named > 0) & (earlier == (slot % CAP).astype(F32))
    return chosen & (slot % (2 * CAP) // CAP == iota((rows, slots), 0) // 2 % 2), expert


def dispatch_kernel(top, yl_ref, tokens_ref, send_ref, held_ref, done):
    peers, block, width = send_ref.shape
    tail = tokens_ref[:, width : width + top].astype(F32)
    chosen, _ = chosen_slots(yl_ref[0], tail, peers * block)
    pick = chosen.astype(F32).astype(BF)
    copies = []
    group = 128 // block
    for part in range(peers // group):
        span = pl.ds(part * group, group)
        lanes = slice(part * 128, (part + 1) * 128)
        sent = dot(pick[:, lanes], tokens_ref[:, :width], ((0,), (0,)))
        held_ref[span] = sent.reshape(group, block, width).astype(BF)
        copy = pltpu.make_async_copy(held_ref.at[span], send_ref.at[span], done.at[part])
        copy.start()
        copies.append(copy)
    for copy in copies:
        copy.wait()


def dispatch(yl, top, tokens, peers, block, width):
    return pl.pallas_call(
        functools.partial(dispatch_kernel, top),
        out_shape=jax.ShapeDtypeStruct((peers, block, width), BF),
        in_specs=[pl.BlockSpec(memory_space=pltpu.SMEM), *vmem(1)],
        out_specs=hbm(),
        scratch_shapes=[
            pltpu.VMEM((peers, block, width), BF),
            pltpu.SemaphoreType.DMA((peers * block // 128,)),
        ],
        compiler_params=PARAMS,
        name="dispatch",
    )(yl, tokens)


def mix_kernel(yl_ref, tail_ref, mix_ref):
    slots = mix_ref.shape[1]
    tail = tail_ref[...].astype(F32)
    top = tail.shape[1] // 2
    sigmoid = jax.nn.sigmoid(tail[:, top:])
    gates = 2.5 * sigmoid / jnp.sum(sigmoid, 1, keepdims=True)
    chosen, expert = chosen_slots(yl_ref[0], tail[:, :top], slots)
    gate = jnp.zeros(chosen.shape, F32)
    for k in range(top):
        gate = jnp.where(tail[:, k : k + 1] == expert, gates[:, k : k + 1], gate)
    high = gate.astype(BF).astype(F32)
    mix = [jnp.where(chosen, part, 0.0) for part in (high, gate - high)]
    mix_ref[...] = jnp.concatenate(mix, 0).astype(BF)


def mixing(yl, tail, slots):
    return pl.pallas_call(
        mix_kernel,
        out_shape=jax.ShapeDtypeStruct((2 * tail.shape[0], slots), BF),
        in_specs=[pl.BlockSpec(memory_space=pltpu.SMEM), *vmem(1)],
        out_specs=vmem(1)[0],
        compiler_params=PARAMS,
        name="mixing",
    )(yl, tail)


def hidden_kernel(rows_ref, own_ref, peer_ref, out_ref, held_ref, done):
    units = own_ref.shape[1] // 2
    rows = rows_ref[...]
    for place, ref in enumerate((own_ref, peer_ref)):
        both = dot(rows, ref[...])
        gate, up = both[:, :units], both[:, units:]
        value = gate / (1.0 + jnp.exp(-gate)) * up
        held_ref[:, place * units : (place + 1) * units] = value.astype(BF)
    copies = [
        pltpu.make_async_copy(held_ref, out_ref.at[peer], done.at[peer])
        for peer in range(out_ref.shape[0])
    ]
    for copy in copies:
        copy.start()
    for copy in copies:
        copy.wait()


def hidden_units(rows, own, peer, peers):
    shape = (rows.shape[0], own.shape[1])
    return pl.pallas_call(
        hidden_kernel,
        out_shape=jax.ShapeDtypeStruct((peers, *shape), BF),
        in_specs=vmem(3),
        out_specs=hbm(),
        scratch_shapes=[pltpu.VMEM(shape, BF), pltpu.SemaphoreType.DMA((peers,))],
        compiler_params=PARAMS,
        name="hidden_units",
    )(rows, own, peer)


def down_kernel(yh_ref, h_ref, own_ref, peer_ref, out_ref):
    total = None
    count = h_ref.shape[0]
    for number in range(count):
        weights = jnp.concatenate([own_ref[number], peer_ref[number]], 0)
        term = dot(h_ref[(yh_ref[0] + count - number) % count], weights)
        total = term if total is None else total + term
    out_ref[...] = total.astype(BF)


def down(yh, h, own, peer):
    return pl.pallas_call(
        down_kernel,
        out_shape=jax.ShapeDtypeStruct((h.shape[1], own.shape[2]), BF),
        in_specs=[pl.BlockSpec(memory_space=pltpu.SMEM), *vmem(3)],
        out_specs=vmem(1)[0],
        compiler_params=PARAMS,
        name="down",
    )(yh.reshape(1), h, own, peer)


def combine_kernel(mix_ref, back_ref, out_ref, held_ref, done):
    peers, requests, _ = out_ref.shape
    rows = peers * requests
    value = dot(mix_ref[...], back_ref[...])
    value = (value[:rows] + value[rows:]).astype(BF)
    for peer in range(peers):
        held_ref[peer] = value[peer * requests : (peer + 1) * requests]
    copy = pltpu.make_async_copy(held_ref, out_ref, done)
    copy.start()
    copy.wait()


def combine(mix, back, requests):
    shape = (mix.shape[0] // 2 // requests, requests, back.shape[1])
    return pl.pallas_call(
        combine_kernel,
        out_shape=jax.ShapeDtypeStruct(shape, BF),
        in_specs=vmem(2),
        out_specs=hbm(),
        scratch_shapes=[pltpu.VMEM(shape, BF), pltpu.SemaphoreType.DMA],
        compiler_params=PARAMS,
        name="combine",
    )(mix, back)


def exchange(x, axes):
    return lax.all_to_all(x, axes, split_axis=0, concat_axis=0, tiled=True)


def shifted(x, axes, by):
    size = lax.axis_size(axes)
    return lax.ppermute(x, axes, [(i, (i + by) % size) for i in range(size)])


def shards(
    latent_cache,
    lengths,
    new_home,
    queries,
    new_latent,
    hidden,
    routes,
    route_logits,
    w_gate,
    w_up,
    w_down,
):
    experts = lax.axis_size(EP)
    yh_size, yl_size = lax.axis_size("yh"), lax.axis_size("yl")
    peers = experts // yl_size
    own_rank = lax.axis_index(EP)
    steps, _, requests, width = hidden.shape
    chunk = width // yh_size
    block = yl_size * CAP
    slots = peers * block

    top = routes.shape[3]
    yl = lax.axis_index("yl").reshape(1)

    packed = pack(hidden, routes, route_logits, yh_size, yl_size)
    tokens = exchange(packed, COLUMN)
    own_w = jnp.concatenate([w_gate[0], w_up[0]], 1)
    served = attend(lengths[own_rank], queries, latent_cache, new_latent)
    tokens, own_w, served0, served1 = lax.optimization_barrier((tokens, own_w, *served))
    tokens = tokens.reshape(-1, tokens.shape[-1])
    send = dispatch(yl, top, tokens, peers, block, width)
    arrived = exchange(send, PLANE).reshape(slots, width)

    far = shifted(served0, EP, experts // 2)
    mix = mixing(yl, tokens[:, width:], slots)
    peer_w = shifted(own_w, "c", 1)
    yh = lax.axis_index("yh")
    sent = [
        lax.dynamic_slice_in_dim(w_down[0], (yh + s) % yh_size * chunk, chunk, 1)
        for s in range(yh_size)
    ]
    own_down = jnp.stack([shifted(x, "yh", s) if s else x for s, x in enumerate(sent)])
    peer_down = shifted(own_down, "c", 1)
    arrived, peer_w, own_down, mix, far = lax.optimization_barrier(
        (arrived, peer_w, own_down, mix, far)
    )
    h = exchange(hidden_units(arrived, own_w, peer_w, yh_size), "yh")
    h, served1 = lax.optimization_barrier((h, served1))
    lower = shifted(served1, EP, 1)
    upper = shifted(served1, EP, -1)
    out = down(yh, h, own_down, peer_down)
    back = exchange(out.reshape(peers, block, chunk), PLANE).reshape(slots, chunk)
    mixed, served1 = lax.optimization_barrier((combine(mix, back, requests), served1))
    final = exchange(mixed, COLUMN)
    final = final.reshape(yh_size, steps, yl_size, requests, chunk).astype(F32)
    final = final.sum(2).astype(BF).transpose(1, 2, 0, 3)

    home = new_home[own_rank]
    result0 = jnp.where(home[0] == own_rank, served0, far)
    result1 = jnp.where(
        home[1] == own_rank,
        served1,
        jnp.where(home[1] == (own_rank + 1) % experts, upper, lower),
    )
    attended = jnp.stack([result0, result1], 1)[:, None]
    return attended, final.reshape(steps, 1, requests, width)


def solution(mesh):
    torus = Mesh(mesh.devices.reshape(4, 2, 2, 4, 8), ("yh", "c", "yl", "x", "z"))
    placed = (
        P(EP, DP, None, None),
        P(None, DP),
        P(None, DP),
        P(None, EP, DP, None, None),
        P(None, EP, DP, None),
        P(None, EP, DP, None),
        P(None, EP, DP, None),
        P(None, EP, DP, None),
        P(EP, None, DP),
        P(EP, None, DP),
        P(EP, DP, None),
    )
    return jax.shard_map(
        shards,
        mesh=torus,
        in_specs=placed,
        out_specs=(P(None, EP, DP, None, None), P(None, EP, DP, None)),
        check_vma=False,
    )
```

```python
import functools

import jax
import jax.numpy as jnp
from jax import lax
from jax.experimental import pallas as pl
from jax.experimental.pallas import tpu as pltpu
from jax.sharding import Mesh
from jax.sharding import PartitionSpec as P

KV_RANK = 512
HEAD_QK = 192
CAP = 4
EP = ("yl", "x", "z")
DP = ("yh", "c")
COLUMN = ("yh", "c", "yl")
PLANE = ("z", "x")
BF = jnp.bfloat16
F32 = jnp.float32
ALL_VMEM = pltpu.CompilerParams(vmem_limit_bytes=60 * 1024 * 1024)
PARAMS = pltpu.CompilerParams(vmem_limit_bytes=48 * 1024 * 1024)


def dot(a, b, dims=((1,), (0,))):
    return lax.dot_general(a, b, (dims, ((), ())), preferred_element_type=F32)


def iota(shape, dim):
    return lax.broadcasted_iota(jnp.int32, shape, dim)


def vmem(n):
    return [pl.BlockSpec(memory_space=pltpu.VMEM)] * n


def attend_kernel(len_ref, query_ref, cache_ref, fresh_ref, out0_ref, out1_ref, keys_ref):
    steps, _, requests, heads, width = query_ref.shape
    cached = cache_ref.shape[2]
    total = keys_ref.shape[0]
    rows = steps * heads
    column = iota((rows, total), 1)
    row_step = iota((rows, total), 0) // heads
    for request, out_ref in zip(range(requests), (out0_ref, out1_ref)):
        keys_ref[:cached] = cache_ref[0, request]
        place = iota((total - cached, width), 0)
        tail = jnp.zeros((total - cached, width), F32)
        for step in range(steps):
            row = fresh_ref[step, 0, request : request + 1, :].astype(F32)
            tail = jnp.where(place == step, row, tail)
        keys_ref[cached:] = tail.astype(BF)
        query = query_ref[:, 0, request].reshape(rows, width)
        keys = keys_ref[...]
        scores = dot(query, keys, ((1,), (1,))) * (HEAD_QK**-0.5)
        old = column < len_ref[request]
        new = (column >= cached) & (column - cached <= row_step)
        scores = jnp.where(old | new, scores, -jnp.inf)
        weights = jnp.exp(scores - jnp.max(scores, 1, keepdims=True))
        probs = (weights / jnp.sum(weights, 1, keepdims=True)).astype(BF)
        served = dot(probs, keys[:, :KV_RANK]).astype(BF)
        out_ref[...] = served.reshape(steps, heads, KV_RANK)


def attend(length, queries, cache, fresh):
    steps, _, _, heads, width = queries.shape
    out = jax.ShapeDtypeStruct((steps, heads, KV_RANK), BF)
    return pl.pallas_call(
        attend_kernel,
        out_shape=(out, out),
        in_specs=[pl.BlockSpec(memory_space=pltpu.SMEM), *vmem(3)],
        out_specs=tuple(vmem(2)),
        scratch_shapes=[pltpu.VMEM((cache.shape[2] + 128, width), BF)],
        compiler_params=PARAMS,
        name="attend",
    )(length, queries, cache, fresh)


def hbm():
    return pl.BlockSpec(memory_space=pltpu.HBM)


def pack_kernel(inner, hidden_ref, routes_ref, logits_ref, out_ref, *scratch):
    hidden_now, routes_now, logits_now, rows_ref, done = scratch
    pairs = ((hidden_ref, hidden_now), (routes_ref, routes_now), (logits_ref, logits_now))
    loads = [
        pltpu.make_async_copy(source, target, done.at[number])
        for number, (source, target) in enumerate(pairs)
    ]
    for load in loads:
        load.start()
    for load in loads:
        load.wait()
    steps, _, _, width = hidden_ref.shape
    for step in range(steps):
        parts = (routes_now[step, 0].astype(F32), logits_now[step, 0].astype(F32))
        tail = jnp.concatenate(parts, -1).astype(BF)
        for place in range(inner):
            rows_ref[step * inner + place, :, :width] = hidden_now[step, 0]
            rows_ref[step * inner + place, :, width:] = tail
    size = steps * inner
    stores = [
        pltpu.make_async_copy(rows_ref, out_ref.at[pl.ds(first, size)], done.at[first // size])
        for first in range(0, out_ref.shape[0], size)
    ]
    for store in stores:
        store.start()
    for store in stores:
        store.wait()


def pack(hidden, routes, logits, outer, inner):
    steps, _, requests, width = hidden.shape
    block = (requests, width + routes.shape[3] + logits.shape[3])
    return pl.pallas_call(
        functools.partial(pack_kernel, inner),
        out_shape=jax.ShapeDtypeStruct((outer * steps * inner, *block), BF),
        in_specs=[hbm()] * 3,
        out_specs=hbm(),
        scratch_shapes=[
            pltpu.VMEM(hidden.shape, BF),
            pltpu.VMEM(routes.shape, routes.dtype),
            pltpu.VMEM(logits.shape, BF),
            pltpu.VMEM((steps * inner, *block), BF),
            pltpu.SemaphoreType.DMA((max(outer, 3),)),
        ],
        compiler_params=ALL_VMEM,
        name="pack",
    )(hidden, routes, logits)


def chosen_slots(columns, yl, tail, slots):
    rows, top = tail.shape
    slot = iota((rows, slots), 1)
    peers = slots // (2 * CAP)
    peer = slot // (2 * CAP)
    expert = yl * peers + peer % columns * (peers // columns) + peer // columns
    expert = expert.astype(F32)
    named = jnp.zeros((rows, slots), F32)
    for k in range(top):
        named = jnp.where(tail[:, k : k + 1] == expert, 1.0, named)
    this, other = iota((rows, rows), 0), iota((rows, rows), 1)
    before = ((other < this) & (other // 2 % 2 == this // 2 % 2)).astype(F32)
    earlier = dot(before.astype(BF), named.astype(BF))
    chosen = (named > 0) & (earlier == (slot % CAP).astype(F32))
    return chosen & (slot % (2 * CAP) // CAP == iota((rows, slots), 0) // 2 % 2), expert


def dispatch_kernel(columns, top, yl_ref, tokens_ref, send_ref, held_ref, done):
    peers, block, width = send_ref.shape
    tail = tokens_ref[:, width : width + top].astype(F32)
    chosen, _ = chosen_slots(columns, yl_ref[0], tail, peers * block)
    pick = chosen.astype(F32).astype(BF)
    copies = []
    group = 128 // block
    for part in range(peers // group):
        span = pl.ds(part * group, group)
        lanes = slice(part * 128, (part + 1) * 128)
        sent = dot(pick[:, lanes], tokens_ref[:, :width], ((0,), (0,)))
        held_ref[span] = sent.reshape(group, block, width).astype(BF)
        copy = pltpu.make_async_copy(held_ref.at[span], send_ref.at[span], done.at[part])
        copy.start()
        copies.append(copy)
    for copy in copies:
        copy.wait()


def dispatch(columns, yl, top, tokens, peers, block, width):
    return pl.pallas_call(
        functools.partial(dispatch_kernel, columns, top),
        out_shape=jax.ShapeDtypeStruct((peers, block, width), BF),
        in_specs=[pl.BlockSpec(memory_space=pltpu.SMEM), *vmem(1)],
        out_specs=hbm(),
        scratch_shapes=[
            pltpu.VMEM((peers, block, width), BF),
            pltpu.SemaphoreType.DMA((peers * block // 128,)),
        ],
        compiler_params=PARAMS,
        name="dispatch",
    )(yl, tokens)


def mix_kernel(columns, yl_ref, tail_ref, mix_ref):
    slots = mix_ref.shape[1]
    tail = tail_ref[...].astype(F32)
    top = tail.shape[1] // 2
    sigmoid = jax.nn.sigmoid(tail[:, top:])
    gates = 2.5 * sigmoid / jnp.sum(sigmoid, 1, keepdims=True)
    chosen, expert = chosen_slots(columns, yl_ref[0], tail[:, :top], slots)
    gate = jnp.zeros(chosen.shape, F32)
    for k in range(top):
        gate = jnp.where(tail[:, k : k + 1] == expert, gates[:, k : k + 1], gate)
    high = gate.astype(BF).astype(F32)
    mix = [jnp.where(chosen, part, 0.0) for part in (high, gate - high)]
    mix_ref[...] = jnp.concatenate(mix, 0).astype(BF)


def mixing(columns, yl, tail, slots):
    return pl.pallas_call(
        functools.partial(mix_kernel, columns),
        out_shape=jax.ShapeDtypeStruct((2 * tail.shape[0], slots), BF),
        in_specs=[pl.BlockSpec(memory_space=pltpu.SMEM), *vmem(1)],
        out_specs=vmem(1)[0],
        compiler_params=PARAMS,
        name="mixing",
    )(yl, tail)


def hidden_kernel(rows_ref, own_ref, peer_ref, out_ref, held_ref, done):
    units = own_ref.shape[1] // 2
    rows = rows_ref[...]
    for place, ref in enumerate((own_ref, peer_ref)):
        both = dot(rows, ref[...])
        gate, up = both[:, :units], both[:, units:]
        value = gate / (1.0 + jnp.exp(-gate)) * up
        held_ref[:, place * units : (place + 1) * units] = value.astype(BF)
    copies = [
        pltpu.make_async_copy(held_ref, out_ref.at[peer], done.at[peer])
        for peer in range(out_ref.shape[0])
    ]
    for copy in copies:
        copy.start()
    for copy in copies:
        copy.wait()


def hidden_units(rows, own, peer, peers):
    shape = (rows.shape[0], own.shape[1])
    return pl.pallas_call(
        hidden_kernel,
        out_shape=jax.ShapeDtypeStruct((peers, *shape), BF),
        in_specs=vmem(3),
        out_specs=hbm(),
        scratch_shapes=[pltpu.VMEM(shape, BF), pltpu.SemaphoreType.DMA((peers,))],
        compiler_params=PARAMS,
        name="hidden_units",
    )(rows, own, peer)


def down_kernel(yh_ref, h_ref, own_ref, peer_ref, out_ref):
    total = None
    count = h_ref.shape[0]
    for number in range(count):
        weights = jnp.concatenate([own_ref[number], peer_ref[number]], 0)
        term = dot(h_ref[(yh_ref[0] + count - number) % count], weights)
        total = term if total is None else total + term
    out_ref[...] = total.astype(BF)


def down(yh, h, own, peer):
    return pl.pallas_call(
        down_kernel,
        out_shape=jax.ShapeDtypeStruct((h.shape[1], own.shape[2]), BF),
        in_specs=[pl.BlockSpec(memory_space=pltpu.SMEM), *vmem(3)],
        out_specs=vmem(1)[0],
        compiler_params=PARAMS,
        name="down",
    )(yh.reshape(1), h, own, peer)


def combine_kernel(mix_ref, back_ref, out_ref, held_ref, done):
    peers, requests, _ = out_ref.shape
    rows = peers * requests
    value = dot(mix_ref[...], back_ref[...])
    value = (value[:rows] + value[rows:]).astype(BF)
    for peer in range(peers):
        held_ref[peer] = value[peer * requests : (peer + 1) * requests]
    copy = pltpu.make_async_copy(held_ref, out_ref, done)
    copy.start()
    copy.wait()


def combine(mix, back, requests):
    shape = (mix.shape[0] // 2 // requests, requests, back.shape[1])
    return pl.pallas_call(
        combine_kernel,
        out_shape=jax.ShapeDtypeStruct(shape, BF),
        in_specs=vmem(2),
        out_specs=hbm(),
        scratch_shapes=[pltpu.VMEM(shape, BF), pltpu.SemaphoreType.DMA],
        compiler_params=PARAMS,
        name="combine",
    )(mix, back)


def exchange(x, axes):
    return lax.all_to_all(x, axes, split_axis=0, concat_axis=0, tiled=True)


def shifted(x, axes, by):
    size = lax.axis_size(axes)
    return lax.ppermute(x, axes, [(i, (i + by) % size) for i in range(size)])


def shards(
    latent_cache,
    lengths,
    new_home,
    queries,
    new_latent,
    hidden,
    routes,
    route_logits,
    w_gate,
    w_up,
    w_down,
):
    experts = lax.axis_size(EP)
    yh_size, yl_size = lax.axis_size("yh"), lax.axis_size("yl")
    peers = experts // yl_size
    own_rank = lax.axis_index(EP)
    steps, _, requests, width = hidden.shape
    chunk = width // yh_size
    block = yl_size * CAP
    slots = peers * block

    top = routes.shape[3]
    yl = lax.axis_index("yl").reshape(1)
    columns = lax.axis_size("x")

    packed = pack(hidden, routes, route_logits, yh_size, yl_size)
    tokens = exchange(packed, COLUMN)
    own_w = jnp.concatenate([w_gate[0], w_up[0]], 1)
    served = attend(lengths[own_rank], queries, latent_cache, new_latent)
    tokens, own_w, served0, served1 = lax.optimization_barrier((tokens, own_w, *served))
    tokens = tokens.reshape(-1, tokens.shape[-1])
    send = dispatch(columns, yl, top, tokens, peers, block, width)
    arrived = exchange(send, PLANE).reshape(slots, width)

    far = shifted(served0, EP, experts // 2)
    mix = mixing(columns, yl, tokens[:, width:], slots)
    peer_w = shifted(own_w, "c", 1)
    yh = lax.axis_index("yh")
    sent = [
        lax.dynamic_slice_in_dim(w_down[0], (yh + s) % yh_size * chunk, chunk, 1)
        for s in range(yh_size)
    ]
    own_down = jnp.stack([shifted(x, "yh", s) if s else x for s, x in enumerate(sent)])
    peer_down = shifted(own_down, "c", 1)
    arrived, peer_w, own_down, mix, far = lax.optimization_barrier(
        (arrived, peer_w, own_down, mix, far)
    )
    h = exchange(hidden_units(arrived, own_w, peer_w, yh_size), "yh")
    h, served1 = lax.optimization_barrier((h, served1))
    lower = shifted(served1, EP, 1)
    upper = shifted(served1, EP, -1)
    out = down(yh, h, own_down, peer_down)
    back = exchange(out.reshape(peers, block, chunk), PLANE).reshape(slots, chunk)
    mixed, served1 = lax.optimization_barrier((combine(mix, back, requests), served1))
    final = exchange(mixed, COLUMN)
    final = final.reshape(yh_size, steps, yl_size, requests, chunk).astype(F32)
    final = final.sum(2).astype(BF).transpose(1, 2, 0, 3)

    home = new_home[own_rank]
    result0 = jnp.where(home[0] == own_rank, served0, far)
    result1 = jnp.where(
        home[1] == own_rank,
        served1,
        jnp.where(home[1] == (own_rank + 1) % experts, upper, lower),
    )
    attended = jnp.stack([result0, result1], 1)[:, None]
    return attended, final.reshape(steps, 1, requests, width)


def solution(mesh):
    torus = Mesh(mesh.devices.reshape(4, 2, 2, 4, 8), ("yh", "c", "yl", "x", "z"))
    placed = (
        P(EP, DP, None, None),
        P(None, DP),
        P(None, DP),
        P(None, EP, DP, None, None),
        P(None, EP, DP, None),
        P(None, EP, DP, None),
        P(None, EP, DP, None),
        P(None, EP, DP, None),
        P(EP, None, DP),
        P(EP, None, DP),
        P(EP, DP, None),
    )
    return jax.shard_map(
        shards,
        mesh=torus,
        in_specs=placed,
        out_specs=(P(None, EP, DP, None, None), P(None, EP, DP, None)),
        check_vma=False,
    )
```

```python
import functools

import jax
import jax.numpy as jnp
from jax import lax
from jax.experimental import pallas as pl
from jax.experimental.pallas import tpu as pltpu
from jax.sharding import Mesh
from jax.sharding import PartitionSpec as P

KV_RANK = 512
HEAD_QK = 192
CAP = 4
EP = ("yl", "x", "z")
DP = ("yh", "c")
COLUMN = ("yh", "c", "yl")
PLANE = ("z", "x")
BF = jnp.bfloat16
F32 = jnp.float32
ALL_VMEM = pltpu.CompilerParams(vmem_limit_bytes=60 * 1024 * 1024)
PARAMS = pltpu.CompilerParams(vmem_limit_bytes=48 * 1024 * 1024)


def dot(a, b, dims=((1,), (0,))):
    return lax.dot_general(a, b, (dims, ((), ())), preferred_element_type=F32)


def iota(shape, dim):
    return lax.broadcasted_iota(jnp.int32, shape, dim)


def vmem(n):
    return [pl.BlockSpec(memory_space=pltpu.VMEM)] * n


def attend_kernel(len_ref, query_ref, cache_ref, fresh_ref, out0_ref, out1_ref, keys_ref):
    steps, _, requests, heads, width = query_ref.shape
    cached = cache_ref.shape[2]
    total = keys_ref.shape[0]
    rows = steps * heads
    column = iota((rows, total), 1)
    row_step = iota((rows, total), 0) // heads
    for request, out_ref in zip(range(requests), (out0_ref, out1_ref)):
        keys_ref[:cached] = cache_ref[0, request]
        place = iota((total - cached, width), 0)
        tail = jnp.zeros((total - cached, width), F32)
        for step in range(steps):
            row = fresh_ref[step, 0, request : request + 1, :].astype(F32)
            tail = jnp.where(place == step, row, tail)
        keys_ref[cached:] = tail.astype(BF)
        query = query_ref[:, 0, request].reshape(rows, width)
        keys = keys_ref[...]
        scores = dot(query, keys, ((1,), (1,))) * (HEAD_QK**-0.5)
        old = column < len_ref[request]
        new = (column >= cached) & (column - cached <= row_step)
        scores = jnp.where(old | new, scores, -jnp.inf)
        weights = jnp.exp(scores - jnp.max(scores, 1, keepdims=True))
        probs = (weights / jnp.sum(weights, 1, keepdims=True)).astype(BF)
        served = dot(probs, keys[:, :KV_RANK]).astype(BF)
        out_ref[...] = served.reshape(steps, heads, KV_RANK)


def attend(length, queries, cache, fresh):
    steps, _, _, heads, width = queries.shape
    out = jax.ShapeDtypeStruct((steps, heads, KV_RANK), BF)
    return pl.pallas_call(
        attend_kernel,
        out_shape=(out, out),
        in_specs=[pl.BlockSpec(memory_space=pltpu.SMEM), *vmem(3)],
        out_specs=tuple(vmem(2)),
        scratch_shapes=[pltpu.VMEM((cache.shape[2] + 128, width), BF)],
        compiler_params=PARAMS,
        name="attend",
    )(length, queries, cache, fresh)


def hbm():
    return pl.BlockSpec(memory_space=pltpu.HBM)


def pack_kernel(inner, hidden_ref, routes_ref, logits_ref, out_ref, *scratch):
    hidden_now, routes_now, logits_now, rows_ref, done = scratch
    pairs = ((hidden_ref, hidden_now), (routes_ref, routes_now), (logits_ref, logits_now))
    loads = [
        pltpu.make_async_copy(source, target, done.at[number])
        for number, (source, target) in enumerate(pairs)
    ]
    for load in loads:
        load.start()
    for load in loads:
        load.wait()
    steps, _, _, width = hidden_ref.shape
    for step in range(steps):
        parts = (routes_now[step, 0].astype(F32), logits_now[step, 0].astype(F32))
        tail = jnp.concatenate(parts, -1).astype(BF)
        for place in range(inner):
            rows_ref[step * inner + place, :, :width] = hidden_now[step, 0]
            rows_ref[step * inner + place, :, width:] = tail
    size = steps * inner
    stores = [
        pltpu.make_async_copy(rows_ref, out_ref.at[pl.ds(first, size)], done.at[first // size])
        for first in range(0, out_ref.shape[0], size)
    ]
    for store in stores:
        store.start()
    for store in stores:
        store.wait()


def pack(hidden, routes, logits, outer, inner):
    steps, _, requests, width = hidden.shape
    block = (requests, width + routes.shape[3] + logits.shape[3])
    return pl.pallas_call(
        functools.partial(pack_kernel, inner),
        out_shape=jax.ShapeDtypeStruct((outer * steps * inner, *block), BF),
        in_specs=[hbm()] * 3,
        out_specs=hbm(),
        scratch_shapes=[
            pltpu.VMEM(hidden.shape, BF),
            pltpu.VMEM(routes.shape, routes.dtype),
            pltpu.VMEM(logits.shape, BF),
            pltpu.VMEM((steps * inner, *block), BF),
            pltpu.SemaphoreType.DMA((max(outer, 3),)),
        ],
        compiler_params=ALL_VMEM,
        name="pack",
    )(hidden, routes, logits)


def chosen_slots(columns, yl, tail, slots):
    rows, top = tail.shape
    slot = iota((rows, slots), 1)
    peers = slots // (2 * CAP)
    peer = slot // (2 * CAP)
    expert = yl * peers + peer % columns * (peers // columns) + peer // columns
    expert = expert.astype(F32)
    named = jnp.zeros((rows, slots), F32)
    for k in range(top):
        named = jnp.where(tail[:, k : k + 1] == expert, 1.0, named)
    this, other = iota((rows, rows), 0), iota((rows, rows), 1)
    before = ((other < this) & (other // 2 % 2 == this // 2 % 2)).astype(F32)
    earlier = dot(before.astype(BF), named.astype(BF))
    chosen = (named > 0) & (earlier == (slot % CAP).astype(F32))
    return chosen & (slot % (2 * CAP) // CAP == iota((rows, slots), 0) // 2 % 2), expert


def dispatch_kernel(columns, top, yl_ref, tokens_ref, send_ref, held_ref, done):
    peers, block, width = send_ref.shape
    tail = tokens_ref[:, width : width + top].astype(F32)
    chosen, _ = chosen_slots(columns, yl_ref[0], tail, peers * block)
    pick = chosen.astype(F32).astype(BF)
    copies = []
    group = 128 // block
    for part in range(peers // group):
        span = pl.ds(part * group, group)
        lanes = slice(part * 128, (part + 1) * 128)
        sent = dot(pick[:, lanes], tokens_ref[:, :width], ((0,), (0,)))
        held_ref[span] = sent.reshape(group, block, width).astype(BF)
        copy = pltpu.make_async_copy(held_ref.at[span], send_ref.at[span], done.at[part])
        copy.start()
        copies.append(copy)
    for copy in copies:
        copy.wait()


def dispatch(columns, yl, top, tokens, peers, block, width):
    return pl.pallas_call(
        functools.partial(dispatch_kernel, columns, top),
        out_shape=jax.ShapeDtypeStruct((peers, block, width), BF),
        in_specs=[pl.BlockSpec(memory_space=pltpu.SMEM), *vmem(1)],
        out_specs=hbm(),
        scratch_shapes=[
            pltpu.VMEM((peers, block, width), BF),
            pltpu.SemaphoreType.DMA((peers * block // 128,)),
        ],
        compiler_params=PARAMS,
        name="dispatch",
    )(yl, tokens)


def mix_kernel(columns, yl_ref, tail_ref, mix_ref):
    slots = mix_ref.shape[1]
    tail = tail_ref[...].astype(F32)
    top = tail.shape[1] // 2
    sigmoid = jax.nn.sigmoid(tail[:, top:])
    gates = 2.5 * sigmoid / jnp.sum(sigmoid, 1, keepdims=True)
    chosen, expert = chosen_slots(columns, yl_ref[0], tail[:, :top], slots)
    gate = jnp.zeros(chosen.shape, F32)
    for k in range(top):
        gate = jnp.where(tail[:, k : k + 1] == expert, gates[:, k : k + 1], gate)
    high = gate.astype(BF).astype(F32)
    mix = [jnp.where(chosen, part, 0.0) for part in (high, gate - high)]
    mix_ref[...] = jnp.concatenate(mix, 0).astype(BF)


def mixing(columns, yl, tail, slots):
    return pl.pallas_call(
        functools.partial(mix_kernel, columns),
        out_shape=jax.ShapeDtypeStruct((2 * tail.shape[0], slots), BF),
        in_specs=[pl.BlockSpec(memory_space=pltpu.SMEM), *vmem(1)],
        out_specs=vmem(1)[0],
        compiler_params=PARAMS,
        name="mixing",
    )(yl, tail)


def hidden_kernel(rows_ref, own_ref, peer_ref, out_ref, held_ref, done):
    units = own_ref.shape[1] // 2
    rows = rows_ref[...]
    for place, ref in enumerate((own_ref, peer_ref)):
        both = dot(rows, ref[...])
        gate, up = both[:, :units], both[:, units:]
        value = gate / (1.0 + jnp.exp(-gate)) * up
        held_ref[:, place * units : (place + 1) * units] = value.astype(BF)
    copies = [
        pltpu.make_async_copy(held_ref, out_ref.at[peer], done.at[peer])
        for peer in range(out_ref.shape[0])
    ]
    for copy in copies:
        copy.start()
    for copy in copies:
        copy.wait()


def hidden_units(rows, own, peer, peers):
    shape = (rows.shape[0], own.shape[1])
    return pl.pallas_call(
        hidden_kernel,
        out_shape=jax.ShapeDtypeStruct((peers, *shape), BF),
        in_specs=vmem(3),
        out_specs=hbm(),
        scratch_shapes=[pltpu.VMEM(shape, BF), pltpu.SemaphoreType.DMA((peers,))],
        compiler_params=PARAMS,
        name="hidden_units",
    )(rows, own, peer)


def down_kernel(yh_ref, h_ref, own_ref, peer_ref, out_ref):
    total = None
    count = h_ref.shape[0]
    for number in range(count):
        weights = jnp.concatenate([own_ref[number], peer_ref[number]], 0)
        term = dot(h_ref[(yh_ref[0] + count - number) % count], weights)
        total = term if total is None else total + term
    out_ref[...] = total.astype(BF)


def down(yh, h, own, peer):
    return pl.pallas_call(
        down_kernel,
        out_shape=jax.ShapeDtypeStruct((h.shape[1], own.shape[2]), BF),
        in_specs=[pl.BlockSpec(memory_space=pltpu.SMEM), *vmem(3)],
        out_specs=vmem(1)[0],
        compiler_params=PARAMS,
        name="down",
    )(yh.reshape(1), h, own, peer)


def combine_kernel(mix_ref, back_ref, out_ref, held_ref, done):
    peers, requests, _ = out_ref.shape
    rows = peers * requests
    value = dot(mix_ref[...], back_ref[...])
    value = (value[:rows] + value[rows:]).astype(BF)
    for peer in range(peers):
        held_ref[peer] = value[peer * requests : (peer + 1) * requests]
    copy = pltpu.make_async_copy(held_ref, out_ref, done)
    copy.start()
    copy.wait()


def combine(mix, back, requests):
    shape = (mix.shape[0] // 2 // requests, requests, back.shape[1])
    return pl.pallas_call(
        combine_kernel,
        out_shape=jax.ShapeDtypeStruct(shape, BF),
        in_specs=vmem(2),
        out_specs=hbm(),
        scratch_shapes=[pltpu.VMEM(shape, BF), pltpu.SemaphoreType.DMA],
        compiler_params=PARAMS,
        name="combine",
    )(mix, back)


def exchange(x, axes):
    return lax.all_to_all(x, axes, split_axis=0, concat_axis=0, tiled=True)


def shifted(x, axes, by):
    size = lax.axis_size(axes)
    return lax.ppermute(x, axes, [(i, (i + by) % size) for i in range(size)])


def shards(
    latent_cache,
    lengths,
    new_home,
    queries,
    new_latent,
    hidden,
    routes,
    route_logits,
    w_gate,
    w_up,
    w_down,
):
    experts = lax.axis_size(EP)
    yh_size, yl_size = lax.axis_size("yh"), lax.axis_size("yl")
    peers = experts // yl_size
    own_rank = lax.axis_index(EP)
    steps, _, requests, width = hidden.shape
    chunk = width // yh_size
    block = yl_size * CAP
    slots = peers * block

    top = routes.shape[3]
    yl = lax.axis_index("yl").reshape(1)
    columns = lax.axis_size("x")

    packed = pack(hidden, routes, route_logits, yh_size, yl_size)
    tokens = exchange(packed, COLUMN)
    own_w = jnp.concatenate([w_gate[0], w_up[0]], 1)
    served = attend(lengths[own_rank], queries, latent_cache, new_latent)
    tokens, own_w, served0, served1 = lax.optimization_barrier((tokens, own_w, *served))
    tokens = tokens.reshape(-1, tokens.shape[-1])
    send = dispatch(columns, yl, top, tokens, peers, block, width)
    arrived = exchange(send, PLANE).reshape(slots, width)

    far = shifted(served0, EP, experts // 2)
    mix = mixing(columns, yl, tokens[:, width:], slots)
    peer_w = shifted(own_w, "c", 1)
    yh = lax.axis_index("yh")
    sent = [
        lax.dynamic_slice_in_dim(w_down[0], (yh + s) % yh_size * chunk, chunk, 1)
        for s in range(yh_size)
    ]
    own_down = jnp.stack([shifted(x, "yh", s) if s else x for s, x in enumerate(sent)])
    peer_down = shifted(own_down, "c", 1)
    arrived, peer_w, own_down, mix, far = lax.optimization_barrier(
        (arrived, peer_w, own_down, mix, far)
    )
    h = hidden_units(arrived, own_w, peer_w, yh_size)
    h, served1 = lax.optimization_barrier((h, served1))
    h = exchange(h, "yh")
    lower = shifted(served1, EP, 1)
    upper = shifted(served1, EP, -1)
    out = down(yh, h, own_down, peer_down)
    out, lower, upper = lax.optimization_barrier((out, lower, upper))
    back = exchange(out.reshape(peers, block, chunk), PLANE).reshape(slots, chunk)
    mixed, served1 = lax.optimization_barrier((combine(mix, back, requests), served1))
    final = exchange(mixed, COLUMN)
    final = final.reshape(yh_size, steps, yl_size, requests, chunk).astype(F32)
    final = final.sum(2).astype(BF).transpose(1, 2, 0, 3)

    home = new_home[own_rank]
    result0 = jnp.where(home[0] == own_rank, served0, far)
    result1 = jnp.where(
        home[1] == own_rank,
        served1,
        jnp.where(home[1] == (own_rank + 1) % experts, upper, lower),
    )
    attended = jnp.stack([result0, result1], 1)[:, None]
    return attended, final.reshape(steps, 1, requests, width)


def solution(mesh):
    torus = Mesh(mesh.devices.reshape(4, 2, 2, 4, 8), ("yh", "c", "yl", "x", "z"))
    placed = (
        P(EP, DP, None, None),
        P(None, DP),
        P(None, DP),
        P(None, EP, DP, None, None),
        P(None, EP, DP, None),
        P(None, EP, DP, None),
        P(None, EP, DP, None),
        P(None, EP, DP, None),
        P(EP, None, DP),
        P(EP, None, DP),
        P(EP, DP, None),
    )
    return jax.shard_map(
        shards,
        mesh=torus,
        in_specs=placed,
        out_specs=(P(None, EP, DP, None, None), P(None, EP, DP, None)),
        check_vma=False,
    )
```
